512 devices in a mesh: inst: 8 (over z_hi, x), space: 64 (over z_lo, y, core).
Axes of the slice: x: 4, y: 8, z: 8 (z_hi: 2, z_lo: 4; z = z_hi * 4 + z_lo), core: 2. Of those that a mesh axis runs over, the one named last changes fastest.
Arguments:
- objective_grad: float32 [16, 5, 131072], P('inst', None, 'space'), may hold values from -6 to 6
- face_jacobians: bfloat16 [16, 6, 5, 5, 131072], P('inst', None, None, None, 'space'), may hold values from -0.75 to 0.75
- plane_jacobians: bfloat16 [16, 5, 5, 8192], P('inst', None, None, 'space'), may hold values from -2 to 2
- diagonal_inverse: float32 [16, 5, 5, 131072], P('inst', None, None, 'space'), as said below
- neighbours: int32 [6, 131072], P(None, 'space'), may hold values from 0 to 2303, as said below
- plane_source: int32 [64], P('space'), may hold values from 0 to 63, each once
Outputs:
- adjoint: float32 [16, 5, 131072], P('inst', None, 'space')
The draws below stay inside these ranges and needn't reach their ends.
Inputs may be any that keep to these rules, and one draw needn't show every extreme that they name: `neighbours`: every neighbour index lies within one block row of 128 cells of the cell itself: from i % 2048 to i % 2048 + 256. `plane_source`: each index appears once. `diagonal_inverse`: each 5x5 block has its diagonal between 0.5 and 1.1 and off-diagonal entries of size up to about 0.5.
All inputs are finite; a program needn't handle non-finite values.
Results may differ from the reference program's by a relative error of at most 0.0003.
Values sent between devices are 32-bit elements; how exact they have to be, the bound alone decides.
A program may use at most 64 MiB of HBM per device.

```python
import math
import jax
import jax.numpy as jnp
from jax import lax

NT = 16
COMP = 5
FACES = 6
ITERS = 2
C = 2048
NC = 131072
IFC = 8192
N_SPACE = 64


def draw_diagonal_inverse(key, part):
    key = jax.random.fold_in(key, 7)
    first, second = jax.random.split(key)
    diag = jax.random.uniform(first, (NT, 1, 1, NC), jnp.float32, 0.6, 1.0)
    offdiag = jnp.clip(jax.random.normal(second, (NT, COMP, COMP, NC), jnp.float32) * 0.15, -0.5, 0.5)
    identity = jnp.eye(COMP, dtype=jnp.float32)[None, :, :, None]
    return (identity * diag + (1.0 - identity) * offdiag).astype(jnp.float32)


def draw_neighbours(key, part):
    key = jax.random.fold_in(key, 3)
    offsets = jax.random.randint(key, (FACES, NC), -128, 129, dtype=jnp.int32)
    position = jnp.arange(NC, dtype=jnp.int32) % C
    index = position[None, :] + 128 + offsets
    index = index.at[0, 0].set(0)
    index = index.at[1, NC - 1].set(C + 255)
    return index.astype(jnp.int32)


def block_scale(rng, extent, pieces, smallest, high):
    level = 1.0
    for axis_at, parts in pieces:
        steps = jax.random.uniform(jax.random.fold_in(jax.random.fold_in(rng, 6), axis_at), (parts,), jnp.float32, smallest / len(pieces), high / len(pieces))
        level = level * jnp.repeat(jnp.exp(steps), extent[axis_at] // parts).reshape((-1,) + (1,) * (len(extent) - 1 - axis_at))
    return level


def bell_draw(stream_key, shape, spread, most, cuts=(), kind=jnp.bfloat16):
    entries = jax.random.normal(stream_key, shape, jnp.float32) * spread
    if len(cuts) > 0:
        entries = block_scale(stream_key, shape, cuts, -0.22, 0.18) * entries
    return jnp.clip(entries, min=-most, max=most).astype(kind)


def setup_inputs(seed: int = 0) -> dict:
    arg_keys = jax.random.split(jax.random.key(seed), 7)
    return {
        "objective_grad": bell_draw(arg_keys[0], (NT, COMP, NC), 1.0, 6.0, ((0, 8), (2, 64)), jnp.float32),
        "face_jacobians": bell_draw(arg_keys[1], (NT, FACES, COMP, COMP, NC), 60 ** -0.5, 0.75, ((0, 8), (4, 64))),
        "plane_jacobians": bell_draw(arg_keys[2], (NT, COMP, COMP, IFC), 10 ** -0.5, 2.0, ((0, 8), (3, 64))),
        "diagonal_inverse": draw_diagonal_inverse(jax.random.fold_in(arg_keys[6], 71), 0),
        "neighbours": draw_neighbours(jax.random.fold_in(arg_keys[6], 71), 0),
        "plane_source": jax.random.permutation(arg_keys[5], N_SPACE).astype(jnp.int32),
    }


frequency = 0.05


def spectral_matrix(count):
    rows = jnp.arange(count)[:, None]
    cols = jnp.arange(count)[None, :]
    diff = (rows - cols).astype(jnp.float32)
    parity = 1.0 - 2.0 * jnp.mod(rows - cols, 2).astype(jnp.float32)
    same = rows == cols
    safe = jnp.where(same, 1.0, jnp.tan(math.pi * diff / count))
    return jnp.where(same, 0.0, 0.5 * parity / safe).astype(jnp.float32)


def apply_inverse(inverse, values):
    return jnp.sum(inverse * values[:, :, None, :], axis=1)


def reference(objective_grad, face_jacobians, plane_jacobians, diagonal_inverse, neighbours, plane_source):
    cellpos = jnp.arange(NC, dtype=jnp.int32)
    group = cellpos // C
    global_nb = jnp.mod(group[None, :] * C + neighbours - 128, NC).astype(jnp.int32)
    rowpos = jnp.arange(IFC, dtype=jnp.int32)
    target = (rowpos // 128) * C + rowpos % 128
    source = plane_source[rowpos // 128] * C + rowpos % 128
    coupling = spectral_matrix(NT)
    adjoint = apply_inverse(diagonal_inverse, objective_grad)
    for sweep_no in range(ITERS):
        summed = jnp.zeros_like(adjoint)
        for face in range(FACES):
            beside = adjoint[:, :, global_nb[face]]
            summed = summed + jnp.sum(face_jacobians[:, face].astype(jnp.float32) * beside[:, :, None, :], axis=1)
        plane_term = jnp.sum(plane_jacobians.astype(jnp.float32) * adjoint[:, :, source][:, :, None, :], axis=1)
        summed = summed.at[:, :, target].add(plane_term)
        spectral = jnp.einsum('mn,mbi->nbi', coupling, adjoint, precision=lax.Precision.HIGHEST)
        adjoint = apply_inverse(diagonal_inverse, objective_grad - summed - frequency * spectral)
    return adjoint
```

```python
import functools
import math

import jax
import jax.numpy as jnp
from jax import lax
from jax.experimental import pallas as pl
from jax.experimental.pallas import tpu as pltpu
from jax.sharding import PartitionSpec as P

MESH = pl.DeviceIdType.MESH
F32 = jnp.float32

ITERS = 2
NT = 16
COMP = 5
FACES = 6
FREQUENCY = 0.05

ROWS = 32
CHUNKS = 4
TOP = 8


def spectral(diff):
    diff = diff % NT
    if diff == 0:
        return 0.0
    return FREQUENCY * 0.5 * (-1.0) ** diff / math.tan(math.pi * diff / NT)


def pick(position, values):
    out = jnp.float32(values[-1])
    for i in range(len(values) - 1):
        out = jnp.where(position == i, jnp.float32(values[i]), out)
    return out


def kernel(
    grad_hbm, face_hbm, plane_hbm, inv_hbm, nb_hbm, src_ref, out_hbm,
    grad, face, plane, inv, nb, lane, side, win, summed, own, xbuf, zsend, zrecv,
    edge, halo, prow, psend, pcol, tab,
    load_sem, xs_sem, xr_sem, zs_sem, zr_sem, hs_sem, hr_sem, as_sem, ar_sem, bs_sem, br_sem, ts_sem, tr_sem,
):
    q, d = lax.axis_index("inst"), lax.axis_index("space")
    half, x = q // 4, lax.rem(q, 4)
    zlo, y, core = d // 16, lax.rem(d, 16) // 2, lax.rem(d, 2)
    col = zlo * 2 + core

    loads = [
        pltpu.make_async_copy(src, dst, load_sem.at[i])
        for i, (src, dst) in enumerate(
            [(grad_hbm, grad), (inv_hbm, inv), (nb_hbm, nb), (plane_hbm, plane), (face_hbm, face)]
        )
    ]
    for load in loads:
        load.start()

    def x_peer(i):
        return (half * 4 + lax.rem(x + i, 4), d)

    z_peer = (lax.rem(q + 4, 8), d)
    before, after = (q, lax.rem(d + 63, 64)), (q, lax.rem(d + 1, 64))

    def y_peer(i):
        return (q, zlo * 16 + lax.rem(y + i, 8) * 2 + core)

    def col_of(i):
        return lax.rem(col + i, 8)

    def col_peer(i):
        other = col_of(i)
        return (q, other // 2 * 16 + y * 2 + lax.rem(other, 2))

    partners = [x_peer(i) for i in (1, 2, 3)] + [z_peer, before, after]
    partners += [y_peer(i) for i in range(1, 8)] + [col_peer(i) for i in range(1, 8)]
    barrier = pltpu.get_barrier_semaphore()
    for p in partners:
        pl.semaphore_signal(barrier, inc=1, device_id=p, device_id_type=MESH)

    def x_copy(s, i, j):
        rows = pl.ds(8 * j, 8)
        return pltpu.make_async_remote_copy(
            src_ref=xbuf.at[s, x, :, rows], dst_ref=xbuf.at[s, x, :, rows],
            send_sem=xs_sem.at[s, i, j], recv_sem=xr_sem.at[s, x, j],
            device_id=x_peer(i), device_id_type=MESH,
        )

    def x_arrival(s, i, j):
        rows, slot = pl.ds(8 * j, 8), lax.rem(x + i, 4)
        return pltpu.make_async_remote_copy(
            src_ref=xbuf.at[s, slot, :, rows], dst_ref=xbuf.at[s, slot, :, rows],
            send_sem=xs_sem.at[s, i, j], recv_sem=xr_sem.at[s, slot, j],
            device_id=x_peer(i), device_id_type=MESH,
        )

    def z_copy(s, j):
        rows = pl.ds(8 * j, 8)
        return pltpu.make_async_remote_copy(
            src_ref=zsend.at[s, :, rows], dst_ref=zrecv.at[s, :, rows],
            send_sem=zs_sem.at[s, j], recv_sem=zr_sem.at[s, j],
            device_id=z_peer, device_id_type=MESH,
        )

    def halo_copy(s, e):
        return pltpu.make_async_remote_copy(
            src_ref=edge.at[s, e], dst_ref=halo.at[s, 1 - e],
            send_sem=hs_sem.at[s, e], recv_sem=hr_sem.at[s, 1 - e],
            device_id=after if e else before, device_id_type=MESH,
        )

    def row_copy(s, i, slot):
        return pltpu.make_async_remote_copy(
            src_ref=edge.at[s, 0], dst_ref=prow.at[s, slot],
            send_sem=as_sem.at[s, i], recv_sem=ar_sem.at[s, slot],
            device_id=y_peer(i), device_id_type=MESH,
        )

    def col_copy(s, i, slot):
        return pltpu.make_async_remote_copy(
            src_ref=psend.at[s, i], dst_ref=pcol.at[s, slot],
            send_sem=bs_sem.at[s, i], recv_sem=br_sem.at[s, slot],
            device_id=col_peer(i), device_id_type=MESH,
        )

    def tab_copy(i, slot):
        return pltpu.make_async_remote_copy(
            src_ref=tab.at[8], dst_ref=tab.at[slot],
            send_sem=ts_sem.at[i], recv_sem=tr_sem.at[slot],
            device_id=col_peer(i), device_id_type=MESH,
        )

    odd = lax.rem(lax.broadcasted_iota(jnp.int32, (8, 128), 0), 2) == 1
    coef = []
    for base in (0, 8):
        straight, crossed = [], []
        for other in range(4):
            steps = [2 * (other - me) + base for me in range(4)]
            straight.append(pick(x, [spectral(e) for e in steps]))
            crossed.append(
                jnp.where(odd, pick(x, [spectral(e + 1) for e in steps]), pick(x, [spectral(e - 1) for e in steps]))
            )
        coef.append((straight, crossed))

    def swap(v):
        return jnp.where(odd, pltpu.roll(v, 1, 0), pltpu.roll(v, 7, 0))

    def publish(s, j, value):
        for c in range(COMP):
            win[s, c, pl.ds(TOP + 8 * j, 8), :] = value[c]
            xbuf[s, x, c, pl.ds(8 * j, 8), :] = value[c]
        if s == 0 and j == 0:
            pl.semaphore_wait(barrier, len(partners))
            for i in range(1, 8):
                tab_copy(i, col).start()
        if j == 0:
            for c in range(COMP):
                edge[s, 0, 2 * c : 2 * c + 2, :] = value[c][0:2]
            prow[s, y] = edge[s, 0]
            for i in range(1, 8):
                row_copy(s, i, y).start()
            halo_copy(s, 0).start()
        if j == CHUNKS - 1:
            for c in range(COMP):
                edge[s, 1, 2 * c : 2 * c + 2, :] = value[c][6:8]
            halo_copy(s, 1).start()
        for i in (2, 1, 3):
            x_copy(s, i, j).start()

    def apply_inverse(j, values):
        rows = pl.ds(8 * j, 8)
        out = []
        for c in range(COMP):
            total = inv[0, c, rows, :] * values[0]
            for b in range(1, COMP):
                total = total + inv[b, c, rows, :] * values[b]
            out.append(total)
        return out

    def faces(s, j):
        rows = pl.ds(8 * j, 8)
        tall = pl.ds(16 * (j // 2), 16)
        lower = 8 * (j % 2)

        def one_face(k, total):
            at, where = lane[k, rows, :], side[k, rows, :]
            total = list(total)
            for a in range(COMP):
                got = [
                    jnp.take_along_axis(
                        win[s, a, pl.ds(TOP + 8 * j + 2 * o, 8), :], at, axis=1, mode="promise_in_bounds"
                    )
                    for o in (-1, 0, 1)
                ]
                beside = jnp.where(where == 0, got[0], jnp.where(where == 1, got[1], got[2]))
                for b in range(COMP):
                    jac = face[k, a, b, tall, :].astype(F32)[lower : lower + 8]
                    total[b] = total[b] + jac * beside
            return tuple(total)

        total = lax.fori_loop(0, FACES, one_face, tuple(jnp.zeros((8, 128), F32) for _ in range(COMP)))
        for b in range(COMP):
            summed[b, rows, :] = total[b]

    def instances(s, j):
        rows = pl.ds(8 * j, 8)
        for i in (1, 3, 2):
            x_arrival(s, i, j).wait_recv()
        for a in range(COMP):
            values = [xbuf[s, other, a, rows, :] for other in range(4)]
            sums = []
            for straight, crossed in coef:
                plain = straight[0] * values[0]
                turned = crossed[0] * values[0]
                for other in range(1, 4):
                    plain = plain + straight[other] * values[other]
                    turned = turned + crossed[other] * values[other]
                sums.append(plain + swap(turned))
            own[a, rows, :] = sums[0]
            zsend[s, a, rows, :] = sums[1]
        z_copy(s, j).start()

    tab[8] = jnp.full((1, 128), src_ref[0], jnp.int32)
    tab[col] = jnp.full((1, 128), src_ref[0], jnp.int32)
    loads[0].wait()
    loads[1].wait()
    for j in range(CHUNKS):
        publish(0, j, apply_inverse(j, [grad[b, pl.ds(8 * j, 8), :] for b in range(COMP)]))

    loads[2].wait()
    for k in range(FACES):
        for block in range(ROWS // 2):
            index = nb[k : k + 1, 128 * block : 128 * block + 128] - 128 * block
            lane[k, 2 * block : 2 * block + 2, :] = jnp.broadcast_to(index & 127, (2, 128))
            side[k, 2 * block : 2 * block + 2, :] = jnp.broadcast_to(index >> 7, (2, 128))
    loads[3].wait()
    loads[4].wait()

    out_copies = []
    for s in range(ITERS):
        for j in (1, 2):
            faces(s, j)
        for j in range(CHUNKS):
            instances(s, j)

        for i in range(1, 8):
            slot = lax.rem(y + i, 8)
            row_copy(s, i, slot).wait_recv()
        if s == 0:
            for i in range(1, 8):
                tab_copy(i, col_of(i)).wait_recv()
        blocks = [prow[s, r] for r in range(8)]
        for i in range(8):
            want = jnp.broadcast_to(lax.rem(tab[col_of(i)], 16) // 2, (16, 128))
            chosen = blocks[7]
            for r in range(7):
                chosen = jnp.where(want == r, blocks[r], chosen)
            if i == 0:
                pcol[s, col] = chosen
            else:
                psend[s, i] = chosen
                col_copy(s, i, col).start()

        for e in (0, 1):
            halo_copy(s, e).wait_recv()
        for c in range(COMP):
            win[s, c, TOP - 2 : TOP, :] = halo[s, 0, 2 * c : 2 * c + 2, :]
            win[s, c, TOP + ROWS : TOP + ROWS + 2, :] = halo[s, 1, 2 * c : 2 * c + 2, :]
        for j in (0, 3):
            faces(s, j)

        for i in range(1, 8):
            col_copy(s, i, col_of(i)).wait_recv()
        mine = tab[8]
        want = jnp.broadcast_to(mine // 16 * 2 + lax.rem(mine, 2), (16, 128))
        source = pcol[s, 7]
        for r in range(7):
            source = jnp.where(want == r, pcol[s, r], source)
        for b in range(COMP):
            term = summed[b, 0:2, :]
            for a in range(COMP):
                term = term + plane[a, b].astype(F32) * source[2 * a : 2 * a + 2]
            summed[b, 0:2, :] = term

        for j in range(CHUNKS):
            rows = pl.ds(8 * j, 8)
            z_copy(s, j).wait_recv()
            right = [
                grad[b, rows, :] - summed[b, rows, :] - (own[b, rows, :] + zrecv[s, b, rows, :]) for b in range(COMP)
            ]
            value = apply_inverse(j, right)
            if s + 1 < ITERS:
                publish(s + 1, j, value)
            else:
                for c in range(COMP):
                    win[s + 1, c, rows, :] = value[c]
                copy = pltpu.make_async_copy(win.at[s + 1, :, rows], out_hbm.at[:, rows], load_sem.at[j])
                copy.start()
                out_copies.append(copy)

    for i in range(1, 8):
        tab_copy(i, col).wait_send()
    for s in range(ITERS):
        for j in range(CHUNKS):
            for i in (1, 2, 3):
                x_copy(s, i, j).wait_send()
            z_copy(s, j).wait_send()
        for e in (0, 1):
            halo_copy(s, e).wait_send()
        for i in range(1, 8):
            row_copy(s, i, y).wait_send()
            col_copy(s, i, col).wait_send()
    for copy in out_copies:
        copy.wait()


def body(objective_grad, face_jacobians, plane_jacobians, diagonal_inverse, neighbours, plane_source):
    blocks = ROWS // 2
    grad = objective_grad.reshape(2, COMP, blocks, 128).transpose(1, 2, 0, 3).reshape(COMP, ROWS, 128)
    face = face_jacobians.reshape(2, FACES, COMP, COMP, blocks, 128)
    face = face.transpose(1, 2, 3, 4, 0, 5).reshape(FACES, COMP, COMP, ROWS, 128)
    inv = diagonal_inverse.reshape(2, COMP, COMP, blocks, 128)
    inv = inv.transpose(1, 2, 3, 0, 4).reshape(COMP, COMP, ROWS, 128)
    plane = plane_jacobians.transpose(1, 2, 0, 3)
    anywhere = pl.BlockSpec(memory_space=pl.ANY)
    dma = pltpu.SemaphoreType.DMA
    out = pl.pallas_call(
        kernel,
        out_shape=jax.ShapeDtypeStruct((COMP, ROWS, 128), F32),
        in_specs=[anywhere] * 5 + [pl.BlockSpec(memory_space=pltpu.SMEM)],
        out_specs=anywhere,
        scratch_shapes=[
            pltpu.VMEM((COMP, ROWS, 128), F32),
            pltpu.VMEM((FACES, COMP, COMP, ROWS, 128), jnp.bfloat16),
            pltpu.VMEM((COMP, COMP, 2, 128), jnp.bfloat16),
            pltpu.VMEM((COMP, COMP, ROWS, 128), F32),
            pltpu.VMEM((FACES, 2048), jnp.int32),
            pltpu.VMEM((FACES, ROWS, 128), jnp.int32),
            pltpu.VMEM((FACES, ROWS, 128), jnp.int32),
            pltpu.VMEM((ITERS + 1, COMP, ROWS + 2 * TOP, 128), F32),
            pltpu.VMEM((COMP, ROWS, 128), F32),
            pltpu.VMEM((COMP, ROWS, 128), F32),
            pltpu.VMEM((ITERS, 4, COMP, ROWS, 128), F32),
            pltpu.VMEM((ITERS, COMP, ROWS, 128), F32),
            pltpu.VMEM((ITERS, COMP, ROWS, 128), F32),
            pltpu.VMEM((ITERS, 2, 16, 128), F32),
            pltpu.VMEM((ITERS, 2, 16, 128), F32),
            pltpu.VMEM((ITERS, 8, 16, 128), F32),
            pltpu.VMEM((ITERS, 8, 16, 128), F32),
            pltpu.VMEM((ITERS, 8, 16, 128), F32),
            pltpu.VMEM((9, 1, 128), jnp.int32),
            dma((5,)),
            dma((ITERS, 4, CHUNKS)), dma((ITERS, 4, CHUNKS)),
            dma((ITERS, CHUNKS)), dma((ITERS, CHUNKS)),
            dma((ITERS, 2)), dma((ITERS, 2)),
            dma((ITERS, 8)), dma((ITERS, 8)),
            dma((ITERS, 8)), dma((ITERS, 8)),
            dma((8,)), dma((8,)),
        ],
        compiler_params=pltpu.CompilerParams(
            collective_id=0, has_side_effects=True, vmem_limit_bytes=48 * 1024 * 1024
        ),
    )(grad, face, plane, inv, neighbours, plane_source)
    return out.reshape(COMP, blocks, 2, 128).transpose(2, 0, 1, 3).reshape(2, COMP, 2048)


def solution(mesh):
    placed = (
        P("inst", None, "space"),
        P("inst", None, None, None, "space"),
        P("inst", None, None, "space"),
        P("inst", None, None, "space"),
        P(None, "space"),
        P("space"),
    )
    return jax.shard_map(
        body, mesh=mesh, in_specs=placed, out_specs=P("inst", None, "space"), check_vma=False
    )
```

```python
import functools
import math

import jax
import jax.numpy as jnp
from jax import lax
from jax.experimental import pallas as pl
from jax.experimental.pallas import tpu as pltpu
from jax.sharding import PartitionSpec as P

MESH = pl.DeviceIdType.MESH
F32 = jnp.float32

ITERS = 2
NT = 16
COMP = 5
FACES = 6
FREQUENCY = 0.05

ROWS = 32
CHUNKS = 4
TOP = 8


def spectral(diff):
    diff = diff % NT
    if diff == 0:
        return 0.0
    return FREQUENCY * 0.5 * (-1.0) ** diff / math.tan(math.pi * diff / NT)


def pick(position, values):
    out = jnp.float32(values[-1])
    for i in range(len(values) - 1):
        out = jnp.where(position == i, jnp.float32(values[i]), out)
    return out


def kernel(
    grad_hbm, face_hbm, plane_hbm, inv_hbm, nb_hbm, src_ref, out_hbm,
    grad, face, plane, inv, nb, lane, side, win, summed, own, xbuf, zsend, zrecv,
    edge, halo, prow, psend, pcol, tab,
    load_sem, xs_sem, xr_sem, zs_sem, zr_sem, hs_sem, hr_sem, as_sem, ar_sem, bs_sem, br_sem, ts_sem, tr_sem,
):
    q, d = lax.axis_index("inst"), lax.axis_index("space")
    half, x = q // 4, lax.rem(q, 4)
    zlo, y, core = d // 16, lax.rem(d, 16) // 2, lax.rem(d, 2)
    col = zlo * 2 + core

    loads = [
        pltpu.make_async_copy(src, dst, load_sem.at[i])
        for i, (src, dst) in enumerate(
            [(grad_hbm, grad), (inv_hbm, inv), (nb_hbm, nb), (plane_hbm, plane), (face_hbm, face)]
        )
    ]
    for load in loads:
        load.start()

    def x_peer(i):
        return (half * 4 + lax.rem(x + i, 4), d)

    z_peer = (lax.rem(q + 4, 8), d)
    before, after = (q, lax.rem(d + 63, 64)), (q, lax.rem(d + 1, 64))

    def y_peer(i):
        return (q, zlo * 16 + lax.rem(y + i, 8) * 2 + core)

    def col_of(i):
        return lax.rem(col + i, 8)

    def col_peer(i):
        other = col_of(i)
        return (q, other // 2 * 16 + y * 2 + lax.rem(other, 2))

    partners = [x_peer(i) for i in (1, 2, 3)] + [z_peer, before, after]
    partners += [y_peer(i) for i in range(1, 8)] + [col_peer(i) for i in range(1, 8)]
    barrier = pltpu.get_barrier_semaphore()
    for p in partners:
        pl.semaphore_signal(barrier, inc=1, device_id=p, device_id_type=MESH)

    def x_copy(s, i, j):
        rows = pl.ds(8 * j, 8)
        return pltpu.make_async_remote_copy(
            src_ref=xbuf.at[s, x, :, rows], dst_ref=xbuf.at[s, x, :, rows],
            send_sem=xs_sem.at[s, i, j], recv_sem=xr_sem.at[s, x, j],
            device_id=x_peer(i), device_id_type=MESH,
        )

    def x_arrival(s, i, j):
        rows, slot = pl.ds(8 * j, 8), lax.rem(x + i, 4)
        return pltpu.make_async_remote_copy(
            src_ref=xbuf.at[s, slot, :, rows], dst_ref=xbuf.at[s, slot, :, rows],
            send_sem=xs_sem.at[s, i, j], recv_sem=xr_sem.at[s, slot, j],
            device_id=x_peer(i), device_id_type=MESH,
        )

    def z_copy(s, j):
        rows = pl.ds(8 * j, 8)
        return pltpu.make_async_remote_copy(
            src_ref=zsend.at[s, :, rows], dst_ref=zrecv.at[s, :, rows],
            send_sem=zs_sem.at[s, j], recv_sem=zr_sem.at[s, j],
            device_id=z_peer, device_id_type=MESH,
        )

    def halo_copy(s, e):
        return pltpu.make_async_remote_copy(
            src_ref=edge.at[s, e], dst_ref=halo.at[s, 1 - e],
            send_sem=hs_sem.at[s, e], recv_sem=hr_sem.at[s, 1 - e],
            device_id=after if e else before, device_id_type=MESH,
        )

    def row_copy(s, i, slot):
        return pltpu.make_async_remote_copy(
            src_ref=edge.at[s, 0], dst_ref=prow.at[s, slot],
            send_sem=as_sem.at[s, i], recv_sem=ar_sem.at[s, slot],
            device_id=y_peer(i), device_id_type=MESH,
        )

    def col_copy(s, i, slot):
        return pltpu.make_async_remote_copy(
            src_ref=psend.at[s, i], dst_ref=pcol.at[s, slot],
            send_sem=bs_sem.at[s, i], recv_sem=br_sem.at[s, slot],
            device_id=col_peer(i), device_id_type=MESH,
        )

    def tab_copy(i, slot):
        return pltpu.make_async_remote_copy(
            src_ref=tab.at[8], dst_ref=tab.at[slot],
            send_sem=ts_sem.at[i], recv_sem=tr_sem.at[slot],
            device_id=col_peer(i), device_id_type=MESH,
        )

    odd = lax.rem(lax.broadcasted_iota(jnp.int32, (8, 128), 0), 2) == 1
    coef = []
    for base in (0, 8):
        straight, crossed = [], []
        for other in range(4):
            steps = [2 * (other - me) + base for me in range(4)]
            straight.append(pick(x, [spectral(e) for e in steps]))
            crossed.append(
                jnp.where(odd, pick(x, [spectral(e + 1) for e in steps]), pick(x, [spectral(e - 1) for e in steps]))
            )
        coef.append((straight, crossed))

    def swap(v):
        return jnp.where(odd, pltpu.roll(v, 1, 0), pltpu.roll(v, 7, 0))

    def publish(s, j, value):
        for c in range(COMP):
            win[s, c, pl.ds(TOP + 8 * j, 8), :] = value[c]
            xbuf[s, x, c, pl.ds(8 * j, 8), :] = value[c]
        if s == 0 and j == 0:
            pl.semaphore_wait(barrier, len(partners))
            for i in range(1, 8):
                tab_copy(i, col).start()
        if j == 0:
            for c in range(COMP):
                edge[s, 0, 2 * c : 2 * c + 2, :] = value[c][0:2]
            prow[s, y] = edge[s, 0]
            for i in range(1, 8):
                row_copy(s, i, y).start()
            halo_copy(s, 0).start()
        if j == CHUNKS - 1:
            for c in range(COMP):
                edge[s, 1, 2 * c : 2 * c + 2, :] = value[c][6:8]
            halo_copy(s, 1).start()
        for i in (2, 1, 3):
            x_copy(s, i, j).start()

    def apply_inverse(j, values):
        rows = pl.ds(8 * j, 8)
        out = []
        for c in range(COMP):
            total = inv[0, c, rows, :] * values[0]
            for b in range(1, COMP):
                total = total + inv[b, c, rows, :] * values[b]
            out.append(total)
        return out

    def faces(s, j):
        rows = pl.ds(8 * j, 8)
        tall = pl.ds(16 * (j // 2), 16)
        lower = 8 * (j % 2)

        def one_face(k, total):
            at, where = lane[k, rows, :], side[k, rows, :]
            total = list(total)
            for a in range(COMP):
                got = [
                    jnp.take_along_axis(
                        win[s, a, pl.ds(TOP + 8 * j + 2 * o, 8), :], at, axis=1, mode="promise_in_bounds"
                    )
                    for o in (-1, 0, 1)
                ]
                beside = jnp.where(where == 0, got[0], jnp.where(where == 1, got[1], got[2]))
                for b in range(COMP):
                    jac = face[k, a, b, tall, :].astype(F32)[lower : lower + 8]
                    total[b] = total[b] + jac * beside
            return tuple(total)

        total = lax.fori_loop(0, FACES, one_face, tuple(jnp.zeros((8, 128), F32) for _ in range(COMP)), unroll=True)
        for b in range(COMP):
            summed[b, rows, :] = total[b]

    def instances(s, j):
        rows = pl.ds(8 * j, 8)
        for i in (1, 3, 2):
            x_arrival(s, i, j).wait_recv()
        for a in range(COMP):
            values = [xbuf[s, other, a, rows, :] for other in range(4)]
            sums = []
            for straight, crossed in coef:
                plain = straight[0] * values[0]
                turned = crossed[0] * values[0]
                for other in range(1, 4):
                    plain = plain + straight[other] * values[other]
                    turned = turned + crossed[other] * values[other]
                sums.append(plain + swap(turned))
            own[a, rows, :] = sums[0]
            zsend[s, a, rows, :] = sums[1]
        z_copy(s, j).start()

    tab[8] = jnp.full((1, 128), src_ref[0], jnp.int32)
    tab[col] = jnp.full((1, 128), src_ref[0], jnp.int32)
    loads[0].wait()
    loads[1].wait()
    for j in range(CHUNKS):
        publish(0, j, apply_inverse(j, [grad[b, pl.ds(8 * j, 8), :] for b in range(COMP)]))

    loads[2].wait()
    for k in range(FACES):
        for block in range(ROWS // 2):
            index = nb[k : k + 1, 128 * block : 128 * block + 128] - 128 * block
            lane[k, 2 * block : 2 * block + 2, :] = jnp.broadcast_to(index & 127, (2, 128))
            side[k, 2 * block : 2 * block + 2, :] = jnp.broadcast_to(index >> 7, (2, 128))
    loads[3].wait()
    loads[4].wait()

    out_copies = []
    for s in range(ITERS):
        for j in (1, 2):
            faces(s, j)
        for j in range(CHUNKS):
            instances(s, j)

        for i in range(1, 8):
            slot = lax.rem(y + i, 8)
            row_copy(s, i, slot).wait_recv()
        if s == 0:
            for i in range(1, 8):
                tab_copy(i, col_of(i)).wait_recv()
        blocks = [prow[s, r] for r in range(8)]
        for i in range(8):
            want = jnp.broadcast_to(lax.rem(tab[col_of(i)], 16) // 2, (16, 128))
            chosen = blocks[7]
            for r in range(7):
                chosen = jnp.where(want == r, blocks[r], chosen)
            if i == 0:
                pcol[s, col] = chosen
            else:
                psend[s, i] = chosen
                col_copy(s, i, col).start()

        for e in (0, 1):
            halo_copy(s, e).wait_recv()
        for c in range(COMP):
            win[s, c, TOP - 2 : TOP, :] = halo[s, 0, 2 * c : 2 * c + 2, :]
            win[s, c, TOP + ROWS : TOP + ROWS + 2, :] = halo[s, 1, 2 * c : 2 * c + 2, :]
        for j in (0, 3):
            faces(s, j)

        for i in range(1, 8):
            col_copy(s, i, col_of(i)).wait_recv()
        mine = tab[8]
        want = jnp.broadcast_to(mine // 16 * 2 + lax.rem(mine, 2), (16, 128))
        source = pcol[s, 7]
        for r in range(7):
            source = jnp.where(want == r, pcol[s, r], source)
        for b in range(COMP):
            term = summed[b, 0:2, :]
            for a in range(COMP):
                term = term + plane[a, b].astype(F32) * source[2 * a : 2 * a + 2]
            summed[b, 0:2, :] = term

        for j in range(CHUNKS):
            rows = pl.ds(8 * j, 8)
            z_copy(s, j).wait_recv()
            right = [
                grad[b, rows, :] - summed[b, rows, :] - (own[b, rows, :] + zrecv[s, b, rows, :]) for b in range(COMP)
            ]
            value = apply_inverse(j, right)
            if s + 1 < ITERS:
                publish(s + 1, j, value)
            else:
                for c in range(COMP):
                    win[s + 1, c, rows, :] = value[c]
                copy = pltpu.make_async_copy(win.at[s + 1, :, rows], out_hbm.at[:, rows], load_sem.at[j])
                copy.start()
                out_copies.append(copy)

    for i in range(1, 8):
        tab_copy(i, col).wait_send()
    for s in range(ITERS):
        for j in range(CHUNKS):
            for i in (1, 2, 3):
                x_copy(s, i, j).wait_send()
            z_copy(s, j).wait_send()
        for e in (0, 1):
            halo_copy(s, e).wait_send()
        for i in range(1, 8):
            row_copy(s, i, y).wait_send()
            col_copy(s, i, col).wait_send()
    for copy in out_copies:
        copy.wait()


def body(objective_grad, face_jacobians, plane_jacobians, diagonal_inverse, neighbours, plane_source):
    blocks = ROWS // 2
    grad = objective_grad.reshape(2, COMP, blocks, 128).transpose(1, 2, 0, 3).reshape(COMP, ROWS, 128)
    face = face_jacobians.reshape(2, FACES, COMP, COMP, blocks, 128)
    face = face.transpose(1, 2, 3, 4, 0, 5).reshape(FACES, COMP, COMP, ROWS, 128)
    inv = diagonal_inverse.reshape(2, COMP, COMP, blocks, 128)
    inv = inv.transpose(1, 2, 3, 0, 4).reshape(COMP, COMP, ROWS, 128)
    plane = plane_jacobians.transpose(1, 2, 0, 3)
    anywhere = pl.BlockSpec(memory_space=pl.ANY)
    dma = pltpu.SemaphoreType.DMA
    out = pl.pallas_call(
        kernel,
        out_shape=jax.ShapeDtypeStruct((COMP, ROWS, 128), F32),
        in_specs=[anywhere] * 5 + [pl.BlockSpec(memory_space=pltpu.SMEM)],
        out_specs=anywhere,
        scratch_shapes=[
            pltpu.VMEM((COMP, ROWS, 128), F32),
            pltpu.VMEM((FACES, COMP, COMP, ROWS, 128), jnp.bfloat16),
            pltpu.VMEM((COMP, COMP, 2, 128), jnp.bfloat16),
            pltpu.VMEM((COMP, COMP, ROWS, 128), F32),
            pltpu.VMEM((FACES, 2048), jnp.int32),
            pltpu.VMEM((FACES, ROWS, 128), jnp.int32),
            pltpu.VMEM((FACES, ROWS, 128), jnp.int32),
            pltpu.VMEM((ITERS + 1, COMP, ROWS + 2 * TOP, 128), F32),
            pltpu.VMEM((COMP, ROWS, 128), F32),
            pltpu.VMEM((COMP, ROWS, 128), F32),
            pltpu.VMEM((ITERS, 4, COMP, ROWS, 128), F32),
            pltpu.VMEM((ITERS, COMP, ROWS, 128), F32),
            pltpu.VMEM((ITERS, COMP, ROWS, 128), F32),
            pltpu.VMEM((ITERS, 2, 16, 128), F32),
            pltpu.VMEM((ITERS, 2, 16, 128), F32),
            pltpu.VMEM((ITERS, 8, 16, 128), F32),
            pltpu.VMEM((ITERS, 8, 16, 128), F32),
            pltpu.VMEM((ITERS, 8, 16, 128), F32),
            pltpu.VMEM((9, 1, 128), jnp.int32),
            dma((5,)),
            dma((ITERS, 4, CHUNKS)), dma((ITERS, 4, CHUNKS)),
            dma((ITERS, CHUNKS)), dma((ITERS, CHUNKS)),
            dma((ITERS, 2)), dma((ITERS, 2)),
            dma((ITERS, 8)), dma((ITERS, 8)),
            dma((ITERS, 8)), dma((ITERS, 8)),
            dma((8,)), dma((8,)),
        ],
        compiler_params=pltpu.CompilerParams(
            collective_id=0, has_side_effects=True, vmem_limit_bytes=60 * 1024 * 1024
        ),
    )(grad, face, plane, inv, neighbours, plane_source)
    return out.reshape(COMP, blocks, 2, 128).transpose(2, 0, 1, 3).reshape(2, COMP, 2048)


def solution(mesh):
    placed = (
        P("inst", None, "space"),
        P("inst", None, None, None, "space"),
        P("inst", None, None, "space"),
        P("inst", None, None, "space"),
        P(None, "space"),
        P("space"),
    )
    return jax.shard_map(
        body, mesh=mesh, in_specs=placed, out_specs=P("inst", None, "space"), check_vma=False
    )
```

```python
import functools
import math

import jax
import jax.numpy as jnp
from jax import lax
from jax.experimental import pallas as pl
from jax.experimental.pallas import tpu as pltpu
from jax.sharding import PartitionSpec as P

MESH = pl.DeviceIdType.MESH
F32 = jnp.float32

ITERS = 2
NT = 16
COMP = 5
FACES = 6
FREQUENCY = 0.05

ROWS = 32
CHUNKS = 4
TOP = 8


def spectral(diff):
    diff = diff % NT
    if diff == 0:
        return 0.0
    return FREQUENCY * 0.5 * (-1.0) ** diff / math.tan(math.pi * diff / NT)


def pick(position, values):
    out = jnp.float32(values[-1])
    for i in range(len(values) - 1):
        out = jnp.where(position == i, jnp.float32(values[i]), out)
    return out


def kernel(
    grad_hbm, face_hbm, plane_hbm, inv_hbm, nb_hbm, src_ref, out_ref,
    grad, face, plane, inv, nb, lane, side, win, summed, own, xbuf, zsend, zrecv,
    edge, halo, prow, psend, pcol, ibuf, tab,
    load_sem, xs_sem, xr_sem, zs_sem, zr_sem, hs_sem, hr_sem, as_sem, ar_sem, bs_sem, br_sem, is_sem, ir_sem, ts_sem, tr_sem, met_sem,
):
    q, d = lax.axis_index("inst"), lax.axis_index("space")
    half, x = q // 4, lax.rem(q, 4)
    zlo, y, core = d // 16, lax.rem(d, 16) // 2, lax.rem(d, 2)
    col = zlo * 2 + core

    loads = [
        pltpu.make_async_copy(src, dst, load_sem.at[i])
        for i, (src, dst) in enumerate(
            [(grad_hbm, grad), (inv_hbm, inv), (nb_hbm, nb), (plane_hbm, plane), (face_hbm, face)]
        )
    ]
    for load in loads:
        load.start()

    def x_peer(i):
        return (half * 4 + lax.rem(x + i, 4), d)

    z_peer = (lax.rem(q + 4, 8), d)

    before, after = (q, lax.rem(d + 63, 64)), (q, lax.rem(d + 1, 64))

    def y_peer(i):
        return (q, zlo * 16 + lax.rem(y + i, 8) * 2 + core)

    def col_of(i):
        return lax.rem(col + i, 8)

    def col_peer(i):
        other = col_of(i)
        return (q, other // 2 * 16 + y * 2 + lax.rem(other, 2))

    partners = [x_peer(i) for i in (1, 2, 3)] + [before, after]
    partners += [y_peer(i) for i in range(1, 8)] + [col_peer(i) for i in range(1, 8)]
    across = [((1 - half) * 4 + other, d) for other in range(4)]
    barrier = pltpu.get_barrier_semaphore()
    for p in partners:
        pl.semaphore_signal(barrier, inc=1, device_id=p, device_id_type=MESH)

    @pl.when(half == 0)
    def _():
        for p in across:
            pl.semaphore_signal(barrier, inc=1, device_id=p, device_id_type=MESH)

    def enter():
        @pl.when(half == 0)
        def _():
            pl.semaphore_wait(barrier, len(partners))

        @pl.when(half == 1)
        def _():
            pl.semaphore_wait(barrier, len(partners) + len(across))
            for p in across:
                pl.semaphore_signal(met_sem, inc=1, device_id=p, device_id_type=MESH)

    def x_copy(s, i, j):
        rows = pl.ds(8 * j, 8)
        return pltpu.make_async_remote_copy(
            src_ref=xbuf.at[s, x, :, rows], dst_ref=xbuf.at[s, x, :, rows],
            send_sem=xs_sem.at[s, i, j], recv_sem=xr_sem.at[s, x, j],
            device_id=x_peer(i), device_id_type=MESH,
        )

    def x_arrival(s, i, j):
        rows, slot = pl.ds(8 * j, 8), lax.rem(x + i, 4)
        return pltpu.make_async_remote_copy(
            src_ref=xbuf.at[s, slot, :, rows], dst_ref=xbuf.at[s, slot, :, rows],
            send_sem=xs_sem.at[s, i, j], recv_sem=xr_sem.at[s, slot, j],
            device_id=x_peer(i), device_id_type=MESH,
        )

    def z_copy(s, j):
        rows = pl.ds(8 * j, 8)
        return pltpu.make_async_remote_copy(
            src_ref=zsend.at[s, :, rows], dst_ref=zrecv.at[s, :, rows],
            send_sem=zs_sem.at[s, j], recv_sem=zr_sem.at[s, j],
            device_id=z_peer, device_id_type=MESH,
        )

    def halo_copy(s, e):
        return pltpu.make_async_remote_copy(
            src_ref=edge.at[s, e], dst_ref=halo.at[s, 1 - e],
            send_sem=hs_sem.at[s, e], recv_sem=hr_sem.at[s, 1 - e],
            device_id=after if e else before, device_id_type=MESH,
        )

    def row_copy(s, i, slot):
        return pltpu.make_async_remote_copy(
            src_ref=edge.at[s, 0], dst_ref=prow.at[s, slot],
            send_sem=as_sem.at[s, i], recv_sem=ar_sem.at[s, slot],
            device_id=y_peer(i), device_id_type=MESH,
        )

    def col_copy(s, i, slot):
        return pltpu.make_async_remote_copy(
            src_ref=psend.at[s, i], dst_ref=pcol.at[s, slot],
            send_sem=bs_sem.at[s, i], recv_sem=br_sem.at[s, slot],
            device_id=col_peer(i), device_id_type=MESH,
        )

    def tab_copy(i, slot):
        return pltpu.make_async_remote_copy(
            src_ref=tab.at[8], dst_ref=tab.at[slot],
            send_sem=ts_sem.at[i], recv_sem=tr_sem.at[slot],
            device_id=col_peer(i), device_id_type=MESH,
        )

    odd = lax.rem(lax.broadcasted_iota(jnp.int32, (8, 128), 0), 2) == 1
    coef = []
    for base in (0, 8):
        straight, crossed = [], []
        for other in range(4):
            steps = [2 * (other - me) + base for me in range(4)]
            straight.append(pick(x, [spectral(e) for e in steps]))
            crossed.append(
                jnp.where(odd, pick(x, [spectral(e + 1) for e in steps]), pick(x, [spectral(e - 1) for e in steps]))
            )
        coef.append((straight, crossed))

    tall_odd = lax.rem(lax.broadcasted_iota(jnp.int32, (16, 128), 0), 2) == 1

    def swap(v, mask):
        return jnp.where(mask, pltpu.roll(v, 1, 0), pltpu.roll(v, v.shape[0] - 1, 0))

    def cross_copy(s, other, slot):
        return pltpu.make_async_remote_copy(
            src_ref=edge.at[s, 0], dst_ref=ibuf.at[s, slot],
            send_sem=is_sem.at[s, other], recv_sem=ir_sem.at[s, slot],
            device_id=across[other], device_id_type=MESH,
        )

    def near_copy(s, i, slot):
        return pltpu.make_async_remote_copy(
            src_ref=edge.at[s, 0], dst_ref=ibuf.at[s, slot],
            send_sem=is_sem.at[s, 4 + i], recv_sem=ir_sem.at[s, slot],
            device_id=x_peer(i), device_id_type=MESH,
        )

    def send_across(s):
        for other in range(4):
            cross_copy(s, other, q).start()

    def send_first(s, held):
        if held:
            pl.when(half == 1)(lambda: send_across(s))
        else:
            send_across(s)
        for i in (2, 1, 3):
            near_copy(s, i, q).start()

    def publish_first(s, value):
        for c in range(COMP):
            win[s, c, TOP : TOP + 2, :] = value[c]
            edge[s, 0, 2 * c : 2 * c + 2, :] = value[c]
        if s == 0:
            enter()
        send_first(s, s == 0)
        for i in (4, 3, 5, 2, 6, 1, 7):
            row_copy(s, i, y).start()
        halo_copy(s, 0).start()
        block = edge[s, 0]
        ibuf[s, q] = block
        prow[s, y] = block

    def publish(s, j, value):
        for c in range(COMP):
            if j == 0:
                win[s, c, TOP + 2 : TOP + 8, :] = value[c][2:]
            else:
                win[s, c, pl.ds(TOP + 8 * j, 8), :] = value[c]
            xbuf[s, x, c, pl.ds(8 * j, 8), :] = value[c]
        for i in (2, 1, 3):
            x_copy(s, i, j).start()
        if j == CHUNKS - 1:
            for c in range(COMP):
                edge[s, 1, 2 * c : 2 * c + 2, :] = value[c][6:8]
            halo_copy(s, 1).start()

    def apply_inverse(rows, values):
        out = []
        for c in range(COMP):
            total = inv[0, c, rows, :] * values[0]
            for b in range(1, COMP):
                total = total + inv[b, c, rows, :] * values[b]
            out.append(total)
        return out

    def faces(s, j):
        rows = pl.ds(8 * j, 8)
        tall = pl.ds(16 * (j // 2), 16)
        lower = 8 * (j % 2)

        def one_face(k, total):
            at, where = lane[k, rows, :], side[k, rows, :]
            total = list(total)
            for a in range(COMP):
                got = [
                    jnp.take_along_axis(
                        win[s, a, pl.ds(TOP + 8 * j + 2 * o, 8), :], at, axis=1, mode="promise_in_bounds"
                    )
                    for o in (-1, 0, 1)
                ]
                beside = jnp.where(where == 0, got[0], jnp.where(where == 1, got[1], got[2]))
                for b in range(COMP):
                    jac = face[k, a, b, tall, :].astype(F32)[lower : lower + 8]
                    total[b] = total[b] + jac * beside
            return tuple(total)

        total = lax.fori_loop(0, FACES, one_face, tuple(jnp.zeros((8, 128), F32) for _ in range(COMP)), unroll=True)
        for b in range(COMP):
            summed[b, rows, :] = total[b]

    def instances(s, j, send=True):
        rows = pl.ds(8 * j, 8)
        for i in (1, 3, 2):
            x_arrival(s, i, j).wait_recv()
        for a in range(COMP):
            values = [xbuf[s, other, a, rows, :] for other in range(4)]
            sums = []
            for straight, crossed in coef:
                plain = straight[0] * values[0]
                turned = crossed[0] * values[0]
                for other in range(1, 4):
                    plain = plain + straight[other] * values[other]
                    turned = turned + crossed[other] * values[other]
                sums.append(plain + swap(turned, odd))
            own[a, rows, :] = sums[0]
            zsend[s, a, rows, :] = sums[1]
        if send:
            z_copy(s, j).start()

    tab[8] = jnp.full((1, 128), src_ref[0], jnp.int32)
    tab[col] = jnp.full((1, 128), src_ref[0], jnp.int32)
    loads[0].wait()
    loads[1].wait()
    for j in range(CHUNKS):
        value = apply_inverse(pl.ds(8 * j, 8), [grad[b, pl.ds(8 * j, 8), :] for b in range(COMP)])
        if j == 0:
            publish_first(0, [v[0:2] for v in value])
            for i in range(1, 8):
                tab_copy(i, col).start()
        publish(0, j, value)

    loads[2].wait()
    for k in range(FACES):
        for block in range(ROWS // 2):
            index = nb[k : k + 1, 128 * block : 128 * block + 128] - 128 * block
            lane[k, 2 * block : 2 * block + 2, :] = jnp.broadcast_to(index & 127, (2, 128))
            side[k, 2 * block : 2 * block + 2, :] = jnp.broadcast_to(index >> 7, (2, 128))
    loads[3].wait()
    loads[4].wait()

    def select(s):
        for i in range(1, 8):
            row_copy(s, i, lax.rem(y + i, 8)).wait_recv()
        if s == 0:
            for i in range(1, 8):
                tab_copy(i, col_of(i)).wait_recv()
        blocks = [prow[s, r] for r in range(8)]
        for i in (4, 3, 5, 2, 6, 1, 7, 0):
            want = jnp.broadcast_to((tab[col_of(i)] >> 1) & 7, (16, 128))
            chosen = blocks[7]
            for r in range(7):
                chosen = jnp.where(want == r, blocks[r], chosen)
            if i == 0:
                pcol[s, col] = chosen
            else:
                psend[s, i] = chosen
                col_copy(s, i, col).start()

    def halos(s):
        for e in (0, 1):
            halo_copy(s, e).wait_recv()
        for c in range(COMP):
            win[s, c, TOP - 2 : TOP, :] = halo[s, 0, 2 * c : 2 * c + 2, :]
            win[s, c, TOP + ROWS : TOP + ROWS + 2, :] = halo[s, 1, 2 * c : 2 * c + 2, :]
        for j in (0, 3):
            faces(s, j)

    def finish(s, j):
        rows = pl.ds(8 * j, 8)
        z_copy(s, j).wait_recv()
        right = [
            grad[b, rows, :] - summed[b, rows, :] - (own[b, rows, :] + zrecv[s, b, rows, :]) for b in range(COMP)
        ]
        value = apply_inverse(rows, right)
        if s + 1 < ITERS:
            publish(s + 1, j, value)
        else:
            for c in range(COMP):
                if j == 0:
                    out_ref[c, 2:8, :] = value[c][2:]
                else:
                    out_ref[c, rows, :] = value[c]

    def finish_first(s):
        for i in range(1, 8):
            col_copy(s, i, col_of(i)).wait_recv()
        mine = tab[8]
        want = jnp.broadcast_to((mine >> 4) * 2 + (mine & 1), (16, 128))
        source = pcol[s, 7]
        for r in range(7):
            source = jnp.where(want == r, pcol[s, r], source)
        terms = []
        for b in range(COMP):
            term = grad[b, 0:2, :] - summed[b, 0:2, :]
            for a in range(COMP):
                term = term - plane[a, b].astype(F32) * source[2 * a : 2 * a + 2]
            terms.append(term)
        for i in (1, 3, 2):
            near_copy(s, i, half * 4 + lax.rem(x + i, 4)).wait_recv()
        for other in range(4):
            cross_copy(s, other, (1 - half) * 4 + other).wait_recv()
        plain = jnp.zeros((16, 128), F32)
        turned = jnp.zeros((16, 128), F32)
        for i in range(8):
            block = ibuf[s, lax.rem(q + i, 8)]
            if i:
                plain = plain + spectral(2 * i) * block
            turned = turned + jnp.where(tall_odd, spectral(2 * i + 1), spectral(2 * i - 1)) * block
        coupled = plain + swap(turned, tall_odd)
        first = pl.ds(0, 2)
        value = apply_inverse(first, [terms[b] - coupled[2 * b : 2 * b + 2] for b in range(COMP)])
        if s + 1 < ITERS:
            publish_first(s + 1, value)
        else:
            for c in range(COMP):
                out_ref[c, 0:2, :] = value[c]

    @pl.when(half == 0)
    def _():
        for j in (1, 2):
            faces(0, j)
        for j in range(CHUNKS):
            instances(0, j, send=False)
        select(0)
        halos(0)
        pl.semaphore_wait(met_sem, len(across))
        send_across(0)
        for j in range(CHUNKS):
            z_copy(0, j).start()
        finish_first(0)
        for j in range(CHUNKS):
            finish(0, j)
        select(1)
        for j in (1, 2):
            faces(1, j)
        for j in range(CHUNKS):
            instances(1, j)
        halos(1)
        for j in range(CHUNKS):
            finish(1, j)
        finish_first(1)

    @pl.when(half == 1)
    def _():
        for j in (1, 2):
            faces(0, j)
        for j in (0, 1):
            instances(0, j)
        select(0)
        for j in (2, 3):
            instances(0, j)
        halos(0)
        for j in range(CHUNKS):
            finish(0, j)
        finish_first(0)
        for j in (1, 2):
            faces(1, j)
        for j in range(CHUNKS):
            instances(1, j)
        select(1)
        halos(1)
        finish_first(1)
        for j in range(CHUNKS):
            finish(1, j)

    for i in range(1, 8):
        tab_copy(i, col).wait_send()
    for s in range(ITERS):
        for j in range(CHUNKS):
            for i in (1, 2, 3):
                x_copy(s, i, j).wait_send()
            z_copy(s, j).wait_send()
        for e in (0, 1):
            halo_copy(s, e).wait_send()
        for other in range(4):
            cross_copy(s, other, q).wait_send()
        for i in (1, 2, 3):
            near_copy(s, i, q).wait_send()
        for i in range(1, 8):
            row_copy(s, i, y).wait_send()
            col_copy(s, i, col).wait_send()


def body(objective_grad, face_jacobians, plane_jacobians, diagonal_inverse, neighbours, plane_source):
    blocks = ROWS // 2
    grad = objective_grad.reshape(2, COMP, blocks, 128).transpose(1, 2, 0, 3).reshape(COMP, ROWS, 128)
    face = face_jacobians.reshape(2, FACES, COMP, COMP, blocks, 128)
    face = face.transpose(1, 2, 3, 4, 0, 5).reshape(FACES, COMP, COMP, ROWS, 128)
    inv = diagonal_inverse.reshape(2, COMP, COMP, blocks, 128)
    inv = inv.transpose(1, 2, 3, 0, 4).reshape(COMP, COMP, ROWS, 128)
    plane = plane_jacobians.transpose(1, 2, 0, 3)
    anywhere = pl.BlockSpec(memory_space=pl.ANY)
    dma = pltpu.SemaphoreType.DMA
    out = pl.pallas_call(
        kernel,
        out_shape=jax.ShapeDtypeStruct((COMP, ROWS, 128), F32),
        in_specs=[anywhere] * 5 + [pl.BlockSpec(memory_space=pltpu.SMEM)],
        out_specs=pl.BlockSpec(memory_space=pltpu.VMEM),
        scratch_shapes=[
            pltpu.VMEM((COMP, ROWS, 128), F32),
            pltpu.VMEM((FACES, COMP, COMP, ROWS, 128), jnp.bfloat16),
            pltpu.VMEM((COMP, COMP, 2, 128), jnp.bfloat16),
            pltpu.VMEM((COMP, COMP, ROWS, 128), F32),
            pltpu.VMEM((FACES, 2048), jnp.int32),
            pltpu.VMEM((FACES, ROWS, 128), jnp.int32),
            pltpu.VMEM((FACES, ROWS, 128), jnp.int32),
            pltpu.VMEM((ITERS + 1, COMP, ROWS + 2 * TOP, 128), F32),
            pltpu.VMEM((COMP, ROWS, 128), F32),
            pltpu.VMEM((COMP, ROWS, 128), F32),
            pltpu.VMEM((ITERS, 4, COMP, ROWS, 128), F32),
            pltpu.VMEM((ITERS, COMP, ROWS, 128), F32),
            pltpu.VMEM((ITERS, COMP, ROWS, 128), F32),
            pltpu.VMEM((ITERS, 2, 16, 128), F32),
            pltpu.VMEM((ITERS, 2, 16, 128), F32),
            pltpu.VMEM((ITERS, 8, 16, 128), F32),
            pltpu.VMEM((ITERS, 8, 16, 128), F32),
            pltpu.VMEM((ITERS, 8, 16, 128), F32),
            pltpu.VMEM((ITERS, 8, 16, 128), F32),
            pltpu.VMEM((9, 1, 128), jnp.int32),
            dma((5,)),
            dma((ITERS, 4, CHUNKS)), dma((ITERS, 4, CHUNKS)),
            dma((ITERS, CHUNKS)), dma((ITERS, CHUNKS)),
            dma((ITERS, 2)), dma((ITERS, 2)),
            dma((ITERS, 8)), dma((ITERS, 8)),
            dma((ITERS, 8)), dma((ITERS, 8)),
            dma((ITERS, 8)), dma((ITERS, 8)),
            dma((8,)), dma((8,)),
            pltpu.SemaphoreType.REGULAR,
        ],
        compiler_params=pltpu.CompilerParams(
            collective_id=0, has_side_effects=True, vmem_limit_bytes=60 * 1024 * 1024
        ),
    )(grad, face, plane, inv, neighbours, plane_source)
    return out.reshape(COMP, blocks, 2, 128).transpose(2, 0, 1, 3).reshape(2, COMP, 2048)


def solution(mesh):
    placed = (
        P("inst", None, "space"),
        P("inst", None, None, None, "space"),
        P("inst", None, None, "space"),
        P("inst", None, None, "space"),
        P(None, "space"),
        P("space"),
    )
    return jax.shard_map(
        body, mesh=mesh, in_specs=placed, out_specs=P("inst", None, "space"), check_vma=False
    )
```

```python
import functools
import math

import jax
import jax.numpy as jnp
from jax import lax
from jax.experimental import pallas as pl
from jax.experimental.pallas import tpu as pltpu
from jax.sharding import PartitionSpec as P

MESH = pl.DeviceIdType.MESH
F32 = jnp.float32

ITERS = 2
NT = 16
COMP = 5
FACES = 6
FREQUENCY = 0.05

ROWS = 32
CHUNKS = 4
TOP = 8


def spectral(diff):
    diff = diff % NT
    if diff == 0:
        return 0.0
    return FREQUENCY * 0.5 * (-1.0) ** diff / math.tan(math.pi * diff / NT)


def pick(position, values):
    out = jnp.float32(values[-1])
    for i in range(len(values) - 1):
        out = jnp.where(position == i, jnp.float32(values[i]), out)
    return out


def kernel(
    grad_hbm, face_hbm, plane_hbm, inv_hbm, nb_hbm, src_ref, out_ref,
    grad, face, plane, inv, nb, lane, side, win, summed, own, xbuf, zsend, zrecv,
    edge, halo, prow, psend, pcol, ibuf, tab,
    load_sem, xs_sem, xr_sem, zs_sem, zr_sem, hs_sem, hr_sem, as_sem, ar_sem, bs_sem, br_sem, is_sem, ir_sem, ts_sem, tr_sem, met_sem, mate_sem,
):
    q, d = lax.axis_index("inst"), lax.axis_index("space")
    half, x = q // 4, lax.rem(q, 4)
    zlo, y, core = d // 16, lax.rem(d, 16) // 2, lax.rem(d, 2)
    col = zlo * 2 + core

    loads = [
        pltpu.make_async_copy(src, dst, load_sem.at[i])
        for i, (src, dst) in enumerate(
            [(grad_hbm, grad), (inv_hbm, inv), (nb_hbm, nb), (plane_hbm, plane), (face_hbm, face)]
        )
    ]
    for load in loads:
        load.start()

    def x_peer(i):
        return (half * 4 + lax.rem(x + i, 4), d)

    z_peer = (lax.rem(q + 4, 8), d)

    before, after = (q, lax.rem(d + 63, 64)), (q, lax.rem(d + 1, 64))

    def y_peer(i):
        return (q, zlo * 16 + lax.rem(y + i, 8) * 2 + core)

    def col_of(i):
        return lax.rem(col + i, 8)

    def col_peer(i):
        other = col_of(i)
        return (q, other // 2 * 16 + y * 2 + lax.rem(other, 2))

    across = [((1 - half) * 4 + other, d) for other in range(4)]
    mate = (q, d + 1 - 2 * core)
    barrier = pltpu.get_barrier_semaphore()

    def greet(p):
        pl.semaphore_signal(barrier, inc=1, device_id=p, device_id_type=MESH)

    def even(p):
        return (p[0], p[1] - lax.rem(p[1], 2))

    def odd_one(p):
        return (p[0], p[1] - lax.rem(p[1], 2) + 1)

    for i in (1, 2, 3):
        greet(even(x_peer(i)))

    @pl.when(core == 1)
    def _():
        greet(mate)

    @pl.when(half == 0)
    def _():
        for p in across:
            greet(even(p))

    greet(odd_one(after))
    for i in range(1, 8):
        greet(odd_one(y_peer(i)))
    for i in range(2, 7):
        greet(odd_one(col_peer(i)))

    @pl.when(core == 0)
    def _():
        greet(odd_one(before))
        greet(odd_one(col_peer(1)))
        greet(odd_one(col_peer(7)))

    @pl.when(core == 1)
    def _():
        greet(odd_one(col_peer(1)))

    def tell_mate():
        pl.semaphore_signal(mate_sem, inc=1, device_id=mate, device_id_type=MESH)

    def enter_inst():
        @pl.when(core == 0)
        def _():
            @pl.when(half == 0)
            def _():
                pl.semaphore_wait(barrier, 7)

            @pl.when(half == 1)
            def _():
                pl.semaphore_wait(barrier, 15)
                for p in across:
                    pl.semaphore_signal(met_sem, inc=1, device_id=p, device_id_type=MESH)
                    pl.semaphore_signal(met_sem, inc=1, device_id=(p[0], p[1] + 1), device_id_type=MESH)

            tell_mate()

        @pl.when(core == 1)
        def _():
            pl.semaphore_wait(mate_sem, 1)

    def enter_space():
        @pl.when(core == 1)
        def _():
            pl.semaphore_wait(barrier, 30)
            tell_mate()

        @pl.when(core == 0)
        def _():
            pl.semaphore_wait(mate_sem, 1)

    def x_copy(s, i, j):
        rows = pl.ds(8 * j, 8)
        return pltpu.make_async_remote_copy(
            src_ref=xbuf.at[s, x, :, rows], dst_ref=xbuf.at[s, x, :, rows],
            send_sem=xs_sem.at[s, i, j], recv_sem=xr_sem.at[s, x, j],
            device_id=x_peer(i), device_id_type=MESH,
        )

    def x_arrival(s, i, j):
        rows, slot = pl.ds(8 * j, 8), lax.rem(x + i, 4)
        return pltpu.make_async_remote_copy(
            src_ref=xbuf.at[s, slot, :, rows], dst_ref=xbuf.at[s, slot, :, rows],
            send_sem=xs_sem.at[s, i, j], recv_sem=xr_sem.at[s, slot, j],
            device_id=x_peer(i), device_id_type=MESH,
        )

    def z_copy(s, j):
        rows = pl.ds(8 * j, 8)
        return pltpu.make_async_remote_copy(
            src_ref=zsend.at[s, :, rows], dst_ref=zrecv.at[s, :, rows],
            send_sem=zs_sem.at[s, j], recv_sem=zr_sem.at[s, j],
            device_id=z_peer, device_id_type=MESH,
        )

    def halo_copy(s, e):
        return pltpu.make_async_remote_copy(
            src_ref=edge.at[s, e], dst_ref=halo.at[s, 1 - e],
            send_sem=hs_sem.at[s, e], recv_sem=hr_sem.at[s, 1 - e],
            device_id=after if e else before, device_id_type=MESH,
        )

    def row_copy(s, i, slot):
        return pltpu.make_async_remote_copy(
            src_ref=edge.at[s, 0], dst_ref=prow.at[s, slot],
            send_sem=as_sem.at[s, i], recv_sem=ar_sem.at[s, slot],
            device_id=y_peer(i), device_id_type=MESH,
        )

    def col_copy(s, i, slot):
        return pltpu.make_async_remote_copy(
            src_ref=psend.at[s, i], dst_ref=pcol.at[s, slot],
            send_sem=bs_sem.at[s, i], recv_sem=br_sem.at[s, slot],
            device_id=col_peer(i), device_id_type=MESH,
        )

    def tab_copy(i, slot):
        return pltpu.make_async_remote_copy(
            src_ref=tab.at[8], dst_ref=tab.at[slot],
            send_sem=ts_sem.at[i], recv_sem=tr_sem.at[slot],
            device_id=col_peer(i), device_id_type=MESH,
        )

    odd = lax.rem(lax.broadcasted_iota(jnp.int32, (8, 128), 0), 2) == 1
    coef = []
    for base in (0, 8):
        straight, crossed = [], []
        for other in range(4):
            steps = [2 * (other - me) + base for me in range(4)]
            straight.append(pick(x, [spectral(e) for e in steps]))
            crossed.append(
                jnp.where(odd, pick(x, [spectral(e + 1) for e in steps]), pick(x, [spectral(e - 1) for e in steps]))
            )
        coef.append((straight, crossed))

    tall_odd = lax.rem(lax.broadcasted_iota(jnp.int32, (16, 128), 0), 2) == 1

    def swap(v, mask):
        return jnp.where(mask, pltpu.roll(v, 1, 0), pltpu.roll(v, v.shape[0] - 1, 0))

    def cross_copy(s, other, slot):
        return pltpu.make_async_remote_copy(
            src_ref=edge.at[s, 0], dst_ref=ibuf.at[s, slot],
            send_sem=is_sem.at[s, other], recv_sem=ir_sem.at[s, slot],
            device_id=across[other], device_id_type=MESH,
        )

    def near_copy(s, i, slot):
        return pltpu.make_async_remote_copy(
            src_ref=edge.at[s, 0], dst_ref=ibuf.at[s, slot],
            send_sem=is_sem.at[s, 4 + i], recv_sem=ir_sem.at[s, slot],
            device_id=x_peer(i), device_id_type=MESH,
        )

    def send_across(s):
        for other in range(4):
            cross_copy(s, other, q).start()

    def send_first(s, held):
        if held:
            pl.when(half == 1)(lambda: send_across(s))
        else:
            send_across(s)
        for i in (2, 1, 3):
            near_copy(s, i, q).start()

    def publish_first(s, value):
        for c in range(COMP):
            win[s, c, TOP : TOP + 2, :] = value[c]
            edge[s, 0, 2 * c : 2 * c + 2, :] = value[c]
        if s:
            send_first(s, False)
            send_space(s, 0)
        block = edge[s, 0]
        ibuf[s, q] = block
        prow[s, y] = block

    def send_space(s, e):
        if e == 0:
            for i in (4, 3, 5, 2, 6, 1, 7):
                row_copy(s, i, y).start()
        halo_copy(s, e).start()

    def publish(s, j, value):
        for c in range(COMP):
            if j == 0:
                win[s, c, TOP + 2 : TOP + 8, :] = value[c][2:]
            else:
                win[s, c, pl.ds(TOP + 8 * j, 8), :] = value[c]
            xbuf[s, x, c, pl.ds(8 * j, 8), :] = value[c]
        for i in (2, 1, 3):
            x_copy(s, i, j).start()
        if j == CHUNKS - 1:
            for c in range(COMP):
                edge[s, 1, 2 * c : 2 * c + 2, :] = value[c][6:8]
            if s:
                send_space(s, 1)

    def apply_inverse(rows, values):
        out = []
        for c in range(COMP):
            total = inv[0, c, rows, :] * values[0]
            for b in range(1, COMP):
                total = total + inv[b, c, rows, :] * values[b]
            out.append(total)
        return out

    def faces(s, j):
        rows = pl.ds(8 * j, 8)
        tall = pl.ds(16 * (j // 2), 16)
        lower = 8 * (j % 2)

        def one_face(k, total):
            at, where = lane[k, rows, :], side[k, rows, :]
            total = list(total)
            for a in range(COMP):
                got = [
                    jnp.take_along_axis(
                        win[s, a, pl.ds(TOP + 8 * j + 2 * o, 8), :], at, axis=1, mode="promise_in_bounds"
                    )
                    for o in (-1, 0, 1)
                ]
                beside = jnp.where(where == 0, got[0], jnp.where(where == 1, got[1], got[2]))
                for b in range(COMP):
                    jac = face[k, a, b, tall, :].astype(F32)[lower : lower + 8]
                    total[b] = total[b] + jac * beside
            return tuple(total)

        total = lax.fori_loop(0, FACES, one_face, tuple(jnp.zeros((8, 128), F32) for _ in range(COMP)), unroll=True)
        for b in range(COMP):
            summed[b, rows, :] = total[b]

    def instances(s, j, send=True):
        rows = pl.ds(8 * j, 8)
        for i in (1, 3, 2):
            x_arrival(s, i, j).wait_recv()
        for a in range(COMP):
            values = [xbuf[s, other, a, rows, :] for other in range(4)]
            sums = []
            for straight, crossed in coef:
                plain = straight[0] * values[0]
                turned = crossed[0] * values[0]
                for other in range(1, 4):
                    plain = plain + straight[other] * values[other]
                    turned = turned + crossed[other] * values[other]
                sums.append(plain + swap(turned, odd))
            own[a, rows, :] = sums[0]
            zsend[s, a, rows, :] = sums[1]
        if send:
            z_copy(s, j).start()

    tab[8] = jnp.full((1, 128), src_ref[0], jnp.int32)
    tab[col] = jnp.full((1, 128), src_ref[0], jnp.int32)
    enter_inst()
    loads[0].wait()
    loads[1].wait()
    for j in range(CHUNKS):
        value = apply_inverse(pl.ds(8 * j, 8), [grad[b, pl.ds(8 * j, 8), :] for b in range(COMP)])
        if j == 0:
            publish_first(0, [v[0:2] for v in value])
            send_first(0, True)
        publish(0, j, value)

    enter_space()
    send_space(0, 0)
    send_space(0, 1)
    for i in range(1, 8):
        tab_copy(i, col).start()
    loads[2].wait()
    for k in range(FACES):
        for block in range(ROWS // 2):
            index = nb[k : k + 1, 128 * block : 128 * block + 128] - 128 * block
            lane[k, 2 * block : 2 * block + 2, :] = jnp.broadcast_to(index & 127, (2, 128))
            side[k, 2 * block : 2 * block + 2, :] = jnp.broadcast_to(index >> 7, (2, 128))
    loads[3].wait()
    loads[4].wait()

    def select(s):
        for i in range(1, 8):
            row_copy(s, i, lax.rem(y + i, 8)).wait_recv()
        if s == 0:
            for i in range(1, 8):
                tab_copy(i, col_of(i)).wait_recv()
        blocks = [prow[s, r] for r in range(8)]
        for i in (4, 3, 5, 2, 6, 1, 7, 0):
            want = jnp.broadcast_to((tab[col_of(i)] >> 1) & 7, (16, 128))
            chosen = blocks[7]
            for r in range(7):
                chosen = jnp.where(want == r, blocks[r], chosen)
            if i == 0:
                pcol[s, col] = chosen
            else:
                psend[s, i] = chosen
                col_copy(s, i, col).start()

    def halos(s):
        for e in (0, 1):
            halo_copy(s, e).wait_recv()
        for c in range(COMP):
            win[s, c, TOP - 2 : TOP, :] = halo[s, 0, 2 * c : 2 * c + 2, :]
            win[s, c, TOP + ROWS : TOP + ROWS + 2, :] = halo[s, 1, 2 * c : 2 * c + 2, :]
        for j in (0, 3):
            faces(s, j)

    def finish(s, j):
        rows = pl.ds(8 * j, 8)
        z_copy(s, j).wait_recv()
        right = [
            grad[b, rows, :] - summed[b, rows, :] - (own[b, rows, :] + zrecv[s, b, rows, :]) for b in range(COMP)
        ]
        value = apply_inverse(rows, right)
        if s + 1 < ITERS:
            publish(s + 1, j, value)
        else:
            for c in range(COMP):
                if j == 0:
                    out_ref[c, 2:8, :] = value[c][2:]
                else:
                    out_ref[c, rows, :] = value[c]

    def finish_first(s):
        for i in range(1, 8):
            col_copy(s, i, col_of(i)).wait_recv()
        mine = tab[8]
        want = jnp.broadcast_to((mine >> 4) * 2 + (mine & 1), (16, 128))
        source = pcol[s, 7]
        for r in range(7):
            source = jnp.where(want == r, pcol[s, r], source)
        terms = []
        for b in range(COMP):
            term = grad[b, 0:2, :] - summed[b, 0:2, :]
            for a in range(COMP):
                term = term - plane[a, b].astype(F32) * source[2 * a : 2 * a + 2]
            terms.append(term)
        for i in (1, 3, 2):
            near_copy(s, i, half * 4 + lax.rem(x + i, 4)).wait_recv()
        for other in range(4):
            cross_copy(s, other, (1 - half) * 4 + other).wait_recv()
        plain = jnp.zeros((16, 128), F32)
        turned = jnp.zeros((16, 128), F32)
        for i in range(8):
            block = ibuf[s, lax.rem(q + i, 8)]
            if i:
                plain = plain + spectral(2 * i) * block
            turned = turned + jnp.where(tall_odd, spectral(2 * i + 1), spectral(2 * i - 1)) * block
        coupled = plain + swap(turned, tall_odd)
        first = pl.ds(0, 2)
        value = apply_inverse(first, [terms[b] - coupled[2 * b : 2 * b + 2] for b in range(COMP)])
        if s + 1 < ITERS:
            publish_first(s + 1, value)
        else:
            for c in range(COMP):
                out_ref[c, 0:2, :] = value[c]

    @pl.when(half == 0)
    def _():
        for j in (1, 2):
            faces(0, j)
        for j in range(CHUNKS):
            instances(0, j, send=False)
        select(0)
        halos(0)
        pl.semaphore_wait(met_sem, len(across))
        send_across(0)
        for j in range(CHUNKS):
            z_copy(0, j).start()
        finish_first(0)
        for j in range(CHUNKS):
            finish(0, j)
        for j in (1, 2):
            faces(1, j)
        select(1)
        for j in range(CHUNKS):
            instances(1, j)
        halos(1)
        finish_first(1)
        for j in range(CHUNKS):
            finish(1, j)

    @pl.when(half == 1)
    def _():
        for j in (1, 2):
            faces(0, j)
        for j in range(CHUNKS):
            instances(0, j)
        select(0)
        halos(0)
        for j in range(CHUNKS):
            finish(0, j)
        finish_first(0)
        for j in (1, 2):
            faces(1, j)
        for j in range(CHUNKS):
            instances(1, j)
        select(1)
        halos(1)
        finish_first(1)
        for j in range(CHUNKS):
            finish(1, j)

    for i in range(1, 8):
        tab_copy(i, col).wait_send()
    for s in range(ITERS):
        for j in range(CHUNKS):
            for i in (1, 2, 3):
                x_copy(s, i, j).wait_send()
            z_copy(s, j).wait_send()
        for e in (0, 1):
            halo_copy(s, e).wait_send()
        for other in range(4):
            cross_copy(s, other, q).wait_send()
        for i in (1, 2, 3):
            near_copy(s, i, q).wait_send()
        for i in range(1, 8):
            row_copy(s, i, y).wait_send()
            col_copy(s, i, col).wait_send()


def body(objective_grad, face_jacobians, plane_jacobians, diagonal_inverse, neighbours, plane_source):
    blocks = ROWS // 2
    grad = objective_grad.reshape(2, COMP, blocks, 128).transpose(1, 2, 0, 3).reshape(COMP, ROWS, 128)
    face = face_jacobians.reshape(2, FACES, COMP, COMP, blocks, 128)
    face = face.transpose(1, 2, 3, 4, 0, 5).reshape(FACES, COMP, COMP, ROWS, 128)
    inv = diagonal_inverse.reshape(2, COMP, COMP, blocks, 128)
    inv = inv.transpose(1, 2, 3, 0, 4).reshape(COMP, COMP, ROWS, 128)
    plane = plane_jacobians.transpose(1, 2, 0, 3)
    anywhere = pl.BlockSpec(memory_space=pl.ANY)
    dma = pltpu.SemaphoreType.DMA
    out = pl.pallas_call(
        kernel,
        out_shape=jax.ShapeDtypeStruct((COMP, ROWS, 128), F32),
        in_specs=[anywhere] * 5 + [pl.BlockSpec(memory_space=pltpu.SMEM)],
        out_specs=pl.BlockSpec(memory_space=pltpu.VMEM),
        scratch_shapes=[
            pltpu.VMEM((COMP, ROWS, 128), F32),
            pltpu.VMEM((FACES, COMP, COMP, ROWS, 128), jnp.bfloat16),
            pltpu.VMEM((COMP, COMP, 2, 128), jnp.bfloat16),
            pltpu.VMEM((COMP, COMP, ROWS, 128), F32),
            pltpu.VMEM((FACES, 2048), jnp.int32),
            pltpu.VMEM((FACES, ROWS, 128), jnp.int32),
            pltpu.VMEM((FACES, ROWS, 128), jnp.int32),
            pltpu.VMEM((ITERS + 1, COMP, ROWS + 2 * TOP, 128), F32),
            pltpu.VMEM((COMP, ROWS, 128), F32),
            pltpu.VMEM((COMP, ROWS, 128), F32),
            pltpu.VMEM((ITERS, 4, COMP, ROWS, 128), F32),
            pltpu.VMEM((ITERS, COMP, ROWS, 128), F32),
            pltpu.VMEM((ITERS, COMP, ROWS, 128), F32),
            pltpu.VMEM((ITERS, 2, 16, 128), F32),
            pltpu.VMEM((ITERS, 2, 16, 128), F32),
            pltpu.VMEM((ITERS, 8, 16, 128), F32),
            pltpu.VMEM((ITERS, 8, 16, 128), F32),
            pltpu.VMEM((ITERS, 8, 16, 128), F32),
            pltpu.VMEM((ITERS, 8, 16, 128), F32),
            pltpu.VMEM((9, 1, 128), jnp.int32),
            dma((5,)),
            dma((ITERS, 4, CHUNKS)), dma((ITERS, 4, CHUNKS)),
            dma((ITERS, CHUNKS)), dma((ITERS, CHUNKS)),
            dma((ITERS, 2)), dma((ITERS, 2)),
            dma((ITERS, 8)), dma((ITERS, 8)),
            dma((ITERS, 8)), dma((ITERS, 8)),
            dma((ITERS, 8)), dma((ITERS, 8)),
            dma((8,)), dma((8,)),
            pltpu.SemaphoreType.REGULAR,
            pltpu.SemaphoreType.REGULAR,
        ],
        compiler_params=pltpu.CompilerParams(
            collective_id=0, has_side_effects=True, vmem_limit_bytes=60 * 1024 * 1024
        ),
    )(grad, face, plane, inv, neighbours, plane_source)
    return out.reshape(COMP, blocks, 2, 128).transpose(2, 0, 1, 3).reshape(2, COMP, 2048)


def solution(mesh):
    placed = (
        P("inst", None, "space"),
        P("inst", None, None, None, "space"),
        P("inst", None, None, "space"),
        P("inst", None, None, "space"),
        P(None, "space"),
        P("space"),
    )
    return jax.shard_map(
        body, mesh=mesh, in_specs=placed, out_specs=P("inst", None, "space"), check_vma=False
    )
```

```python
import functools
import math

import jax
import jax.numpy as jnp
from jax import lax
from jax.experimental import pallas as pl
from jax.experimental.pallas import tpu as pltpu
from jax.sharding import PartitionSpec as P

MESH = pl.DeviceIdType.MESH
F32 = jnp.float32

ITERS = 2
NT = 16
COMP = 5
FACES = 6
FREQUENCY = 0.05

ROWS = 32
CHUNKS = 4
TOP = 8


def spectral(diff):
    diff = diff % NT
    if diff == 0:
        return 0.0
    return FREQUENCY * 0.5 * (-1.0) ** diff / math.tan(math.pi * diff / NT)


def pick(position, values):
    out = jnp.float32(values[-1])
    for i in range(len(values) - 1):
        out = jnp.where(position == i, jnp.float32(values[i]), out)
    return out


def kernel(
    grad_hbm, face_hbm, plane_hbm, inv_hbm, nb_hbm, src_ref, out_ref,
    grad, face, plane, inv, nb, lane, side, win, summed, own, xbuf, zsend, zrecv,
    edge, halo, prow, psend, pcol, ibuf, zfirst, zgot, tab,
    load_sem, xs_sem, xr_sem, zs_sem, zr_sem, hs_sem, hr_sem, as_sem, ar_sem, bs_sem, br_sem, is_sem, ir_sem, ts_sem, tr_sem, met_sem, mate_sem, fs_sem, fr_sem,
):
    q, d = lax.axis_index("inst"), lax.axis_index("space")
    half, x = q // 4, lax.rem(q, 4)
    zlo, y, core = d // 16, lax.rem(d, 16) // 2, lax.rem(d, 2)
    col = zlo * 2 + core

    loads = [
        pltpu.make_async_copy(src, dst, load_sem.at[i])
        for i, (src, dst) in enumerate(
            [(grad_hbm, grad), (inv_hbm, inv), (nb_hbm, nb), (plane_hbm, plane), (face_hbm, face)]
        )
    ]
    for load in loads:
        load.start()

    def x_peer(i):
        return (half * 4 + lax.rem(x + i, 4), d)

    z_peer = (lax.rem(q + 4, 8), d)

    before, after = (q, lax.rem(d + 63, 64)), (q, lax.rem(d + 1, 64))

    def y_peer(i):
        return (q, zlo * 16 + lax.rem(y + i, 8) * 2 + core)

    def col_of(i):
        return lax.rem(col + i, 8)

    def col_peer(i):
        other = col_of(i)
        return (q, other // 2 * 16 + y * 2 + lax.rem(other, 2))

    across = [((1 - half) * 4 + other, d) for other in range(4)]
    mate = (q, d + 1 - 2 * core)
    barrier = pltpu.get_barrier_semaphore()

    def greet(p):
        pl.semaphore_signal(barrier, inc=1, device_id=p, device_id_type=MESH)

    def even(p):
        return (p[0], p[1] - lax.rem(p[1], 2))

    def odd_one(p):
        return (p[0], p[1] - lax.rem(p[1], 2) + 1)

    for i in (1, 2, 3):
        greet(even(x_peer(i)))

    @pl.when(core == 1)
    def _():
        greet(mate)

    @pl.when(half == 0)
    def _():
        for p in across:
            greet(even(p))

    greet(odd_one(after))
    for i in range(1, 8):
        greet(odd_one(y_peer(i)))
    for i in range(2, 7):
        greet(odd_one(col_peer(i)))

    @pl.when(core == 0)
    def _():
        greet(odd_one(before))
        greet(odd_one(col_peer(1)))
        greet(odd_one(col_peer(7)))

    @pl.when(core == 1)
    def _():
        greet(odd_one(col_peer(1)))

    def tell_mate():
        pl.semaphore_signal(mate_sem, inc=1, device_id=mate, device_id_type=MESH)

    def enter_inst():
        @pl.when(core == 0)
        def _():
            @pl.when(half == 0)
            def _():
                pl.semaphore_wait(barrier, 7)

            @pl.when(half == 1)
            def _():
                pl.semaphore_wait(barrier, 15)
                pl.semaphore_signal(met_sem, inc=1, device_id=z_peer, device_id_type=MESH)
                pl.semaphore_signal(met_sem, inc=1, device_id=(z_peer[0], d + 1), device_id_type=MESH)

            tell_mate()

        @pl.when(core == 1)
        def _():
            pl.semaphore_wait(mate_sem, 1)

    def enter_space():
        @pl.when(core == 1)
        def _():
            pl.semaphore_wait(barrier, 30)
            tell_mate()

        @pl.when(core == 0)
        def _():
            pl.semaphore_wait(mate_sem, 1)

    def x_copy(s, i, j):
        rows = pl.ds(8 * j, 8)
        return pltpu.make_async_remote_copy(
            src_ref=xbuf.at[s, x, :, rows], dst_ref=xbuf.at[s, x, :, rows],
            send_sem=xs_sem.at[s, i, j], recv_sem=xr_sem.at[s, x, j],
            device_id=x_peer(i), device_id_type=MESH,
        )

    def x_arrival(s, i, j):
        rows, slot = pl.ds(8 * j, 8), lax.rem(x + i, 4)
        return pltpu.make_async_remote_copy(
            src_ref=xbuf.at[s, slot, :, rows], dst_ref=xbuf.at[s, slot, :, rows],
            send_sem=xs_sem.at[s, i, j], recv_sem=xr_sem.at[s, slot, j],
            device_id=x_peer(i), device_id_type=MESH,
        )

    def z_copy(s, j):
        rows = pl.ds(8 * j, 8)
        return pltpu.make_async_remote_copy(
            src_ref=zsend.at[s, :, rows], dst_ref=zrecv.at[s, :, rows],
            send_sem=zs_sem.at[s, j], recv_sem=zr_sem.at[s, j],
            device_id=z_peer, device_id_type=MESH,
        )

    def halo_copy(s, e):
        return pltpu.make_async_remote_copy(
            src_ref=edge.at[s, e], dst_ref=halo.at[s, 1 - e],
            send_sem=hs_sem.at[s, e], recv_sem=hr_sem.at[s, 1 - e],
            device_id=after if e else before, device_id_type=MESH,
        )

    def row_copy(s, i, slot):
        return pltpu.make_async_remote_copy(
            src_ref=edge.at[s, 0], dst_ref=prow.at[s, slot],
            send_sem=as_sem.at[s, i], recv_sem=ar_sem.at[s, slot],
            device_id=col_peer(i), device_id_type=MESH,
        )

    def col_copy(s, i, slot):
        return pltpu.make_async_remote_copy(
            src_ref=psend.at[s, i], dst_ref=pcol.at[s, slot],
            send_sem=bs_sem.at[s, i], recv_sem=br_sem.at[s, slot],
            device_id=y_peer(i), device_id_type=MESH,
        )

    def tab_copy(i, slot):
        return pltpu.make_async_remote_copy(
            src_ref=tab.at[8], dst_ref=tab.at[slot],
            send_sem=ts_sem.at[i], recv_sem=tr_sem.at[slot],
            device_id=y_peer(i), device_id_type=MESH,
        )

    odd = lax.rem(lax.broadcasted_iota(jnp.int32, (8, 128), 0), 2) == 1
    coef = []
    for base in (0, 8):
        straight, crossed = [], []
        for other in range(4):
            steps = [2 * (other - me) + base for me in range(4)]
            straight.append(pick(x, [spectral(e) for e in steps]))
            crossed.append(
                jnp.where(odd, pick(x, [spectral(e + 1) for e in steps]), pick(x, [spectral(e - 1) for e in steps]))
            )
        coef.append((straight, crossed))

    def swap(v, mask):
        return jnp.where(mask, pltpu.roll(v, 1, 0), pltpu.roll(v, v.shape[0] - 1, 0))

    def cross_copy(s, other, slot):
        return pltpu.make_async_remote_copy(
            src_ref=edge.at[s, 0], dst_ref=ibuf.at[s, slot],
            send_sem=is_sem.at[s, other], recv_sem=ir_sem.at[s, slot],
            device_id=across[other], device_id_type=MESH,
        )

    def near_copy(s, i, slot):
        return pltpu.make_async_remote_copy(
            src_ref=edge.at[s, 0], dst_ref=ibuf.at[s, slot],
            send_sem=is_sem.at[s, 4 + i], recv_sem=ir_sem.at[s, slot],
            device_id=x_peer(i), device_id_type=MESH,
        )

    def send_across(s):
        for other in range(4):
            cross_copy(s, other, q).start()

    def send_first(s):
        pl.when(half == 1)(lambda: send_across(s))
        for i in (2, 1, 3):
            near_copy(s, i, q).start()

    def first_copy(s):
        return pltpu.make_async_remote_copy(
            src_ref=zfirst.at[s], dst_ref=zgot.at[s], send_sem=fs_sem.at[s], recv_sem=fr_sem.at[s],
            device_id=z_peer, device_id_type=MESH,
        )

    def first_sum(s, kind, group, h):
        straight, crossed = coef[kind]
        rows = pl.ds(8 * h, 8)
        values = [ibuf[s, 4 * group + other, rows, :] for other in range(4)]
        plain, turned = straight[0] * values[0], crossed[0] * values[0]
        for other in range(1, 4):
            plain = plain + straight[other] * values[other]
            turned = turned + crossed[other] * values[other]
        return plain + swap(turned, odd)

    def near_arrivals(s):
        for i in (1, 3, 2):
            near_copy(s, i, half * 4 + lax.rem(x + i, 4)).wait_recv()

    def first_across(s):
        near_arrivals(s)
        for h in (0, 1):
            zfirst[s, 8 * h : 8 * h + 8, :] = first_sum(s, 1, 0, h)

    def publish_first(s, value):
        for c in range(COMP):
            win[s, c, TOP : TOP + 2, :] = value[c]
            edge[s, 0, 2 * c : 2 * c + 2, :] = value[c]
        if s:
            send_first(s)
            send_space(s, 0)
        block = edge[s, 0]
        ibuf[s, q] = block
        prow[s, col] = block

    def send_space(s, e):
        if e == 0:
            for i in (4, 3, 5, 2, 6, 1, 7):
                row_copy(s, i, col).start()
        halo_copy(s, e).start()

    def publish(s, j, value):
        for c in range(COMP):
            if j == 0:
                win[s, c, TOP + 2 : TOP + 8, :] = value[c][2:]
            else:
                win[s, c, pl.ds(TOP + 8 * j, 8), :] = value[c]
            xbuf[s, x, c, pl.ds(8 * j, 8), :] = value[c]
        for i in (2, 1, 3):
            x_copy(s, i, j).start()
        if j == CHUNKS - 1:
            for c in range(COMP):
                edge[s, 1, 2 * c : 2 * c + 2, :] = value[c][6:8]
            if s:
                send_space(s, 1)

    def apply_inverse(rows, values):
        out = []
        for c in range(COMP):
            total = inv[0, c, rows, :] * values[0]
            for b in range(1, COMP):
                total = total + inv[b, c, rows, :] * values[b]
            out.append(total)
        return out

    def faces(s, j):
        rows = pl.ds(8 * j, 8)
        tall = pl.ds(16 * (j // 2), 16)
        lower = 8 * (j % 2)

        def one_face(k, total):
            at, where = lane[k, rows, :], side[k, rows, :]
            total = list(total)
            for a in range(COMP):
                got = [
                    jnp.take_along_axis(
                        win[s, a, pl.ds(TOP + 8 * j + 2 * o, 8), :], at, axis=1, mode="promise_in_bounds"
                    )
                    for o in (-1, 0, 1)
                ]
                beside = jnp.where(where == 0, got[0], jnp.where(where == 1, got[1], got[2]))
                for b in range(COMP):
                    jac = face[k, a, b, tall, :].astype(F32)[lower : lower + 8]
                    total[b] = total[b] + jac * beside
            return tuple(total)

        total = lax.fori_loop(0, FACES, one_face, tuple(jnp.zeros((8, 128), F32) for _ in range(COMP)), unroll=True)
        for b in range(COMP):
            summed[b, rows, :] = total[b]

    def instances(s, j, send=True):
        rows = pl.ds(8 * j, 8)
        for i in (1, 3, 2):
            x_arrival(s, i, j).wait_recv()
        for a in range(COMP):
            values = [xbuf[s, other, a, rows, :] for other in range(4)]
            sums = []
            for straight, crossed in coef:
                plain = straight[0] * values[0]
                turned = crossed[0] * values[0]
                for other in range(1, 4):
                    plain = plain + straight[other] * values[other]
                    turned = turned + crossed[other] * values[other]
                sums.append(plain + swap(turned, odd))
            own[a, rows, :] = sums[0]
            zsend[s, a, rows, :] = sums[1]
        if send:
            z_copy(s, j).start()

    tab[8] = jnp.full((1, 128), src_ref[0], jnp.int32)
    tab[y] = jnp.full((1, 128), src_ref[0], jnp.int32)
    enter_inst()
    loads[0].wait()
    loads[1].wait()
    for j in range(CHUNKS):
        value = apply_inverse(pl.ds(8 * j, 8), [grad[b, pl.ds(8 * j, 8), :] for b in range(COMP)])
        if j == 0:
            publish_first(0, [v[0:2] for v in value])
            send_first(0)
        publish(0, j, value)

    enter_space()
    send_space(0, 0)
    send_space(0, 1)
    for i in range(1, 8):
        tab_copy(i, y).start()
    loads[2].wait()
    for k in range(FACES):
        for block in range(ROWS // 2):
            index = nb[k : k + 1, 128 * block : 128 * block + 128] - 128 * block
            lane[k, 2 * block : 2 * block + 2, :] = jnp.broadcast_to(index & 127, (2, 128))
            side[k, 2 * block : 2 * block + 2, :] = jnp.broadcast_to(index >> 7, (2, 128))
    loads[3].wait()
    loads[4].wait()

    def select(s):
        for i in range(1, 8):
            row_copy(s, i, col_of(i)).wait_recv()
        if s == 0:
            for i in range(1, 8):
                tab_copy(i, lax.rem(y + i, 8)).wait_recv()
        blocks = [prow[s, r] for r in range(8)]
        for i in (4, 3, 5, 2, 6, 1, 7, 0):
            wanted = tab[lax.rem(y + i, 8)]
            want = jnp.broadcast_to((wanted >> 4) * 2 + (wanted & 1), (16, 128))
            chosen = blocks[7]
            for r in range(7):
                chosen = jnp.where(want == r, blocks[r], chosen)
            if i == 0:
                pcol[s, y] = chosen
            else:
                psend[s, i] = chosen
                col_copy(s, i, y).start()

    def halos(s):
        for e in (0, 1):
            halo_copy(s, e).wait_recv()
        for c in range(COMP):
            win[s, c, TOP - 2 : TOP, :] = halo[s, 0, 2 * c : 2 * c + 2, :]
            win[s, c, TOP + ROWS : TOP + ROWS + 2, :] = halo[s, 1, 2 * c : 2 * c + 2, :]
        for j in (0, 3):
            faces(s, j)

    def finish(s, j):
        rows = pl.ds(8 * j, 8)
        z_copy(s, j).wait_recv()
        right = [
            grad[b, rows, :] - summed[b, rows, :] - (own[b, rows, :] + zrecv[s, b, rows, :]) for b in range(COMP)
        ]
        value = apply_inverse(rows, right)
        if s + 1 < ITERS:
            publish(s + 1, j, value)
        else:
            for c in range(COMP):
                if j == 0:
                    out_ref[c, 2:8, :] = value[c][2:]
                else:
                    out_ref[c, rows, :] = value[c]

    def finish_first(s, upper):
        for i in range(1, 8):
            col_copy(s, i, lax.rem(y + i, 8)).wait_recv()
        mine = tab[8]
        want = jnp.broadcast_to((mine >> 1) & 7, (16, 128))
        source = pcol[s, 7]
        for r in range(7):
            source = jnp.where(want == r, pcol[s, r], source)
        terms = []
        for b in range(COMP):
            term = grad[b, 0:2, :] - summed[b, 0:2, :]
            for a in range(COMP):
                term = term - plane[a, b].astype(F32) * source[2 * a : 2 * a + 2]
            terms.append(term)
        if upper:
            near_arrivals(s)
            first_copy(s).wait_recv()
            coupled = [first_sum(s, 0, 1, h) + zgot[s, 8 * h : 8 * h + 8, :] for h in (0, 1)]
        else:
            for other in range(4):
                cross_copy(s, other, (1 - half) * 4 + other).wait_recv()
            coupled = [first_sum(s, 0, 0, h) + first_sum(s, 1, 1, h) for h in (0, 1)]
        coupled = [coupled[b // 4][2 * b % 8 : 2 * b % 8 + 2] for b in range(COMP)]
        first = pl.ds(0, 2)
        value = apply_inverse(first, [terms[b] - coupled[b] for b in range(COMP)])
        if s + 1 < ITERS:
            publish_first(s + 1, value)
        else:
            for c in range(COMP):
                out_ref[c, 0:2, :] = value[c]

    @pl.when(half == 0)
    def _():
        for j in (1, 2):
            faces(0, j)
        for j in range(CHUNKS):
            instances(0, j, send=False)
        select(0)
        halos(0)
        first_across(0)
        pl.semaphore_wait(met_sem, 1)
        first_copy(0).start()
        for j in range(CHUNKS):
            z_copy(0, j).start()
        finish_first(0, False)
        for j in range(CHUNKS):
            finish(0, j)
        for j in (1, 2):
            faces(1, j)
        select(1)
        first_across(1)
        first_copy(1).start()
        for j in range(CHUNKS):
            instances(1, j)
        halos(1)
        finish_first(1, False)
        for j in range(CHUNKS):
            finish(1, j)

    @pl.when(half == 1)
    def _():
        for j in (1, 2):
            faces(0, j)
        for j in range(CHUNKS):
            instances(0, j)
        select(0)
        halos(0)
        for j in range(CHUNKS):
            finish(0, j)
        finish_first(0, True)
        for j in (1, 2):
            faces(1, j)
        for j in range(CHUNKS):
            instances(1, j)
        select(1)
        halos(1)
        finish_first(1, True)
        for j in range(CHUNKS):
            finish(1, j)

    for i in range(1, 8):
        tab_copy(i, y).wait_send()
    for s in range(ITERS):
        for j in range(CHUNKS):
            for i in (1, 2, 3):
                x_copy(s, i, j).wait_send()
            z_copy(s, j).wait_send()
        for e in (0, 1):
            halo_copy(s, e).wait_send()

        @pl.when(half == 0)
        def _():
            first_copy(s).wait_send()

        @pl.when(half == 1)
        def _():
            for other in range(4):
                cross_copy(s, other, q).wait_send()

        for i in (1, 2, 3):
            near_copy(s, i, q).wait_send()
        for i in range(1, 8):
            row_copy(s, i, col).wait_send()
            col_copy(s, i, y).wait_send()


def body(objective_grad, face_jacobians, plane_jacobians, diagonal_inverse, neighbours, plane_source):
    blocks = ROWS // 2
    grad = objective_grad.reshape(2, COMP, blocks, 128).transpose(1, 2, 0, 3).reshape(COMP, ROWS, 128)
    face = face_jacobians.reshape(2, FACES, COMP, COMP, blocks, 128)
    face = face.transpose(1, 2, 3, 4, 0, 5).reshape(FACES, COMP, COMP, ROWS, 128)
    inv = diagonal_inverse.reshape(2, COMP, COMP, blocks, 128)
    inv = inv.transpose(1, 2, 3, 0, 4).reshape(COMP, COMP, ROWS, 128)
    plane = plane_jacobians.transpose(1, 2, 0, 3)
    anywhere = pl.BlockSpec(memory_space=pl.ANY)
    dma = pltpu.SemaphoreType.DMA
    out = pl.pallas_call(
        kernel,
        out_shape=jax.ShapeDtypeStruct((COMP, ROWS, 128), F32),
        in_specs=[anywhere] * 5 + [pl.BlockSpec(memory_space=pltpu.SMEM)],
        out_specs=pl.BlockSpec(memory_space=pltpu.VMEM),
        scratch_shapes=[
            pltpu.VMEM((COMP, ROWS, 128), F32),
            pltpu.VMEM((FACES, COMP, COMP, ROWS, 128), jnp.bfloat16),
            pltpu.VMEM((COMP, COMP, 2, 128), jnp.bfloat16),
            pltpu.VMEM((COMP, COMP, ROWS, 128), F32),
            pltpu.VMEM((FACES, 2048), jnp.int32),
            pltpu.VMEM((FACES, ROWS, 128), jnp.int32),
            pltpu.VMEM((FACES, ROWS, 128), jnp.int32),
            pltpu.VMEM((ITERS + 1, COMP, ROWS + 2 * TOP, 128), F32),
            pltpu.VMEM((COMP, ROWS, 128), F32),
            pltpu.VMEM((COMP, ROWS, 128), F32),
            pltpu.VMEM((ITERS, 4, COMP, ROWS, 128), F32),
            pltpu.VMEM((ITERS, COMP, ROWS, 128), F32),
            pltpu.VMEM((ITERS, COMP, ROWS, 128), F32),
            pltpu.VMEM((ITERS, 2, 16, 128), F32),
            pltpu.VMEM((ITERS, 2, 16, 128), F32),
            pltpu.VMEM((ITERS, 8, 16, 128), F32),
            pltpu.VMEM((ITERS, 8, 16, 128), F32),
            pltpu.VMEM((ITERS, 8, 16, 128), F32),
            pltpu.VMEM((ITERS, 8, 16, 128), F32),
            pltpu.VMEM((ITERS, 16, 128), F32),
            pltpu.VMEM((ITERS, 16, 128), F32),
            pltpu.VMEM((9, 1, 128), jnp.int32),
            dma((5,)),
            dma((ITERS, 4, CHUNKS)), dma((ITERS, 4, CHUNKS)),
            dma((ITERS, CHUNKS)), dma((ITERS, CHUNKS)),
            dma((ITERS, 2)), dma((ITERS, 2)),
            dma((ITERS, 8)), dma((ITERS, 8)),
            dma((ITERS, 8)), dma((ITERS, 8)),
            dma((ITERS, 8)), dma((ITERS, 8)),
            dma((8,)), dma((8,)),
            pltpu.SemaphoreType.REGULAR,
            pltpu.SemaphoreType.REGULAR,
            dma((ITERS,)), dma((ITERS,)),
        ],
        compiler_params=pltpu.CompilerParams(
            collective_id=0, has_side_effects=True, vmem_limit_bytes=60 * 1024 * 1024
        ),
    )(grad, face, plane, inv, neighbours, plane_source)
    return out.reshape(COMP, blocks, 2, 128).transpose(2, 0, 1, 3).reshape(2, COMP, 2048)


def solution(mesh):
    placed = (
        P("inst", None, "space"),
        P("inst", None, None, None, "space"),
        P("inst", None, None, "space"),
        P("inst", None, None, "space"),
        P(None, "space"),
        P("space"),
    )
    return jax.shard_map(
        body, mesh=mesh, in_specs=placed, out_specs=P("inst", None, "space"), check_vma=False
    )
```

```python
import functools
import math

import jax
import jax.numpy as jnp
from jax import lax
from jax.experimental import pallas as pl
from jax.experimental.pallas import tpu as pltpu
from jax.sharding import PartitionSpec as P

MESH = pl.DeviceIdType.MESH
F32 = jnp.float32

ITERS = 2
NT = 16
COMP = 5
FACES = 6
FREQUENCY = 0.05

ROWS = 32
CHUNKS = 4
TOP = 8


def spectral(diff):
    diff = diff % NT
    if diff == 0:
        return 0.0
    return FREQUENCY * 0.5 * (-1.0) ** diff / math.tan(math.pi * diff / NT)


def pick(position, values):
    out = jnp.float32(values[-1])
    for i in range(len(values) - 1):
        out = jnp.where(position == i, jnp.float32(values[i]), out)
    return out


def kernel(
    grad_hbm, face_hbm, plane_hbm, inv_hbm, nb_hbm, src_ref, out_ref,
    grad, face, plane, inv, nb, lane, side, win, summed, own, xbuf, zsend, zrecv,
    edge, halo, prow, psend, pcol, ibuf, zfirst, zgot, tab,
    load_sem, xs_sem, xr_sem, zs_sem, zr_sem, hs_sem, hr_sem, as_sem, ar_sem, bs_sem, br_sem, is_sem, ir_sem, ts_sem, tr_sem, met_sem, mate_sem, fs_sem, fr_sem,
):
    q, d = lax.axis_index("inst"), lax.axis_index("space")
    half, x = q // 4, lax.rem(q, 4)
    zlo, y, core = d // 16, lax.rem(d, 16) // 2, lax.rem(d, 2)
    col = zlo * 2 + core

    loads = [
        pltpu.make_async_copy(src, dst, load_sem.at[i])
        for i, (src, dst) in enumerate(
            [(grad_hbm, grad), (inv_hbm, inv), (nb_hbm, nb), (plane_hbm, plane), (face_hbm, face)]
        )
    ]
    for load in loads:
        load.start()

    def x_peer(i):
        return (half * 4 + lax.rem(x + i, 4), d)

    z_peer = (lax.rem(q + 4, 8), d)

    before, after = (q, lax.rem(d + 63, 64)), (q, lax.rem(d + 1, 64))

    def y_peer(i):
        return (q, zlo * 16 + lax.rem(y + i, 8) * 2 + core)

    def col_of(i):
        return lax.rem(col + i, 8)

    def col_peer(i):
        other = col_of(i)
        return (q, other // 2 * 16 + y * 2 + lax.rem(other, 2))

    across = [((1 - half) * 4 + other, d) for other in range(4)]
    mate = (q, d + 1 - 2 * core)
    barrier = pltpu.get_barrier_semaphore()

    def greet(p):
        pl.semaphore_signal(barrier, inc=1, device_id=p, device_id_type=MESH)

    def even(p):
        return (p[0], p[1] - lax.rem(p[1], 2))

    def odd_one(p):
        return (p[0], p[1] - lax.rem(p[1], 2) + 1)

    for i in (1, 2, 3):
        greet(even(x_peer(i)))

    @pl.when(core == 1)
    def _():
        greet(mate)

    @pl.when(half == 0)
    def _():
        for p in across:
            greet(even(p))

    greet(odd_one(after))
    for i in range(1, 8):
        greet(odd_one(y_peer(i)))
    for i in range(2, 7):
        greet(odd_one(col_peer(i)))

    @pl.when(core == 0)
    def _():
        greet(odd_one(before))
        greet(odd_one(col_peer(1)))
        greet(odd_one(col_peer(7)))

    @pl.when(core == 1)
    def _():
        greet(odd_one(col_peer(1)))

    def tell_mate():
        pl.semaphore_signal(mate_sem, inc=1, device_id=mate, device_id_type=MESH)

    def enter_inst():
        @pl.when(core == 0)
        def _():
            @pl.when(half == 0)
            def _():
                pl.semaphore_wait(barrier, 7)

            @pl.when(half == 1)
            def _():
                pl.semaphore_wait(barrier, 15)
                pl.semaphore_signal(met_sem, inc=1, device_id=z_peer, device_id_type=MESH)
                pl.semaphore_signal(met_sem, inc=1, device_id=(z_peer[0], d + 1), device_id_type=MESH)

            tell_mate()

        @pl.when(core == 1)
        def _():
            pl.semaphore_wait(mate_sem, 1)

    def enter_space():
        @pl.when(core == 1)
        def _():
            pl.semaphore_wait(barrier, 30)
            tell_mate()

        @pl.when(core == 0)
        def _():
            pl.semaphore_wait(mate_sem, 1)

    def x_copy(s, i, j):
        rows = pl.ds(8 * j, 8)
        return pltpu.make_async_remote_copy(
            src_ref=xbuf.at[s, x, :, rows], dst_ref=xbuf.at[s, x, :, rows],
            send_sem=xs_sem.at[s, i, j], recv_sem=xr_sem.at[s, x, j],
            device_id=x_peer(i), device_id_type=MESH,
        )

    def x_arrival(s, i, j):
        rows, slot = pl.ds(8 * j, 8), lax.rem(x + i, 4)
        return pltpu.make_async_remote_copy(
            src_ref=xbuf.at[s, slot, :, rows], dst_ref=xbuf.at[s, slot, :, rows],
            send_sem=xs_sem.at[s, i, j], recv_sem=xr_sem.at[s, slot, j],
            device_id=x_peer(i), device_id_type=MESH,
        )

    def z_copy(s, j):
        rows = pl.ds(8 * j, 8)
        return pltpu.make_async_remote_copy(
            src_ref=zsend.at[s, :, rows], dst_ref=zrecv.at[s, :, rows],
            send_sem=zs_sem.at[s, j], recv_sem=zr_sem.at[s, j],
            device_id=z_peer, device_id_type=MESH,
        )

    def halo_copy(s, e):
        return pltpu.make_async_remote_copy(
            src_ref=edge.at[s, e], dst_ref=halo.at[s, 1 - e],
            send_sem=hs_sem.at[s, e], recv_sem=hr_sem.at[s, 1 - e],
            device_id=after if e else before, device_id_type=MESH,
        )

    def row_copy(s, i, slot):
        return pltpu.make_async_remote_copy(
            src_ref=edge.at[s, 0], dst_ref=prow.at[s, slot],
            send_sem=as_sem.at[s, i], recv_sem=ar_sem.at[s, slot],
            device_id=col_peer(i), device_id_type=MESH,
        )

    def col_copy(s, i, slot):
        return pltpu.make_async_remote_copy(
            src_ref=psend.at[s, i], dst_ref=pcol.at[s, slot],
            send_sem=bs_sem.at[s, i], recv_sem=br_sem.at[s, slot],
            device_id=y_peer(i), device_id_type=MESH,
        )

    def tab_copy(i, slot):
        return pltpu.make_async_remote_copy(
            src_ref=tab.at[8], dst_ref=tab.at[slot],
            send_sem=ts_sem.at[i], recv_sem=tr_sem.at[slot],
            device_id=y_peer(i), device_id_type=MESH,
        )

    odd = lax.rem(lax.broadcasted_iota(jnp.int32, (8, 128), 0), 2) == 1
    coef = []
    for base in (0, 8):
        straight, crossed = [], []
        for other in range(4):
            steps = [2 * (other - me) + base for me in range(4)]
            straight.append(pick(x, [spectral(e) for e in steps]))
            crossed.append(
                jnp.where(odd, pick(x, [spectral(e + 1) for e in steps]), pick(x, [spectral(e - 1) for e in steps]))
            )
        coef.append((straight, crossed))

    def swap(v, mask):
        return jnp.where(mask, pltpu.roll(v, 1, 0), pltpu.roll(v, v.shape[0] - 1, 0))

    def cross_copy(s, other, slot):
        return pltpu.make_async_remote_copy(
            src_ref=edge.at[s, 0], dst_ref=ibuf.at[s, slot],
            send_sem=is_sem.at[s, other], recv_sem=ir_sem.at[s, slot],
            device_id=across[other], device_id_type=MESH,
        )

    def near_copy(s, i, slot):
        return pltpu.make_async_remote_copy(
            src_ref=edge.at[s, 0], dst_ref=ibuf.at[s, slot],
            send_sem=is_sem.at[s, 4 + i], recv_sem=ir_sem.at[s, slot],
            device_id=x_peer(i), device_id_type=MESH,
        )

    def send_across(s):
        for other in range(4):
            cross_copy(s, other, q).start()

    def send_first(s):
        pl.when(half == 1)(lambda: send_across(s))
        for i in (2, 1, 3):
            near_copy(s, i, q).start()

    def first_copy(s):
        return pltpu.make_async_remote_copy(
            src_ref=zfirst.at[s], dst_ref=zgot.at[s], send_sem=fs_sem.at[s], recv_sem=fr_sem.at[s],
            device_id=z_peer, device_id_type=MESH,
        )

    def first_sum(s, kind, group, h):
        straight, crossed = coef[kind]
        rows = pl.ds(8 * h, 8)
        values = [ibuf[s, 4 * group + other, rows, :] for other in range(4)]
        plain, turned = straight[0] * values[0], crossed[0] * values[0]
        for other in range(1, 4):
            plain = plain + straight[other] * values[other]
            turned = turned + crossed[other] * values[other]
        return plain + swap(turned, odd)

    def near_arrivals(s):
        for i in (1, 3, 2):
            near_copy(s, i, half * 4 + lax.rem(x + i, 4)).wait_recv()

    def first_across(s):
        near_arrivals(s)
        for h in (0, 1):
            zfirst[s, 8 * h : 8 * h + 8, :] = first_sum(s, 1, 0, h)

    def publish_first(s, value):
        for c in range(COMP):
            win[s, c, TOP : TOP + 2, :] = value[c]
            edge[s, 0, 2 * c : 2 * c + 2, :] = value[c]
        if s:
            send_first(s)
            send_space(s, 0)
        block = edge[s, 0]
        ibuf[s, q] = block
        prow[s, col] = block

    def send_space(s, e):
        if e == 0:
            for i in (4, 3, 5, 2, 6, 1, 7):
                row_copy(s, i, col).start()
        halo_copy(s, e).start()

    def publish(s, j, value):
        for c in range(COMP):
            if j == 0:
                win[s, c, TOP + 2 : TOP + 8, :] = value[c][2:]
            else:
                win[s, c, pl.ds(TOP + 8 * j, 8), :] = value[c]
            xbuf[s, x, c, pl.ds(8 * j, 8), :] = value[c]
        for i in (2, 1, 3):
            x_copy(s, i, j).start()
        if j == CHUNKS - 1:
            for c in range(COMP):
                edge[s, 1, 2 * c : 2 * c + 2, :] = value[c][6:8]
            if s:
                send_space(s, 1)

    def apply_inverse(rows, values):
        out = []
        for c in range(COMP):
            total = inv[0, c, rows, :] * values[0]
            for b in range(1, COMP):
                total = total + inv[b, c, rows, :] * values[b]
            out.append(total)
        return out

    def faces(s, j):
        rows = pl.ds(8 * j, 8)
        tall = pl.ds(16 * (j // 2), 16)
        lower = 8 * (j % 2)

        def one_face(k, total):
            at, where = lane[k, rows, :], side[k, rows, :]
            total = list(total)
            for a in range(COMP):
                got = [
                    jnp.take_along_axis(
                        win[s, a, pl.ds(TOP + 8 * j + 2 * o, 8), :], at, axis=1, mode="promise_in_bounds"
                    )
                    for o in (-1, 0, 1)
                ]
                beside = jnp.where(where == 0, got[0], jnp.where(where == 1, got[1], got[2]))
                for b in range(COMP):
                    jac = face[k, a, b, tall, :].astype(F32)[lower : lower + 8]
                    total[b] = total[b] + jac * beside
            return tuple(total)

        total = lax.fori_loop(0, FACES, one_face, tuple(jnp.zeros((8, 128), F32) for _ in range(COMP)), unroll=True)
        for b in range(COMP):
            summed[b, rows, :] = total[b]

    def instances(s, j, send=True):
        rows = pl.ds(8 * j, 8)
        for i in (1, 3, 2):
            x_arrival(s, i, j).wait_recv()
        for a in range(COMP):
            values = [xbuf[s, other, a, rows, :] for other in range(4)]
            sums = []
            for straight, crossed in coef:
                plain = straight[0] * values[0]
                turned = crossed[0] * values[0]
                for other in range(1, 4):
                    plain = plain + straight[other] * values[other]
                    turned = turned + crossed[other] * values[other]
                sums.append(plain + swap(turned, odd))
            own[a, rows, :] = sums[0]
            zsend[s, a, rows, :] = sums[1]
        if send:
            z_copy(s, j).start()

    tab[8] = jnp.full((1, 128), src_ref[0], jnp.int32)
    tab[y] = jnp.full((1, 128), src_ref[0], jnp.int32)
    enter_inst()
    loads[0].wait()
    loads[1].wait()
    for j in range(CHUNKS):
        value = apply_inverse(pl.ds(8 * j, 8), [grad[b, pl.ds(8 * j, 8), :] for b in range(COMP)])
        if j == 0:
            publish_first(0, [v[0:2] for v in value])
            send_first(0)
        publish(0, j, value)

    enter_space()
    send_space(0, 0)
    send_space(0, 1)
    for i in range(1, 8):
        tab_copy(i, y).start()
    loads[2].wait()
    for k in range(FACES):
        for block in range(ROWS // 2):
            index = nb[k : k + 1, 128 * block : 128 * block + 128] - 128 * block
            lane[k, 2 * block : 2 * block + 2, :] = jnp.broadcast_to(index & 127, (2, 128))
            side[k, 2 * block : 2 * block + 2, :] = jnp.broadcast_to(index >> 7, (2, 128))
    loads[3].wait()
    loads[4].wait()

    def select(s):
        for i in range(1, 8):
            row_copy(s, i, col_of(i)).wait_recv()
        if s == 0:
            for i in range(1, 8):
                tab_copy(i, lax.rem(y + i, 8)).wait_recv()
        blocks = [prow[s, r] for r in range(8)]
        for i in (4, 3, 5, 2, 6, 1, 7, 0):
            wanted = tab[lax.rem(y + i, 8)]
            want = jnp.broadcast_to((wanted >> 4) * 2 + (wanted & 1), (16, 128))
            chosen = blocks[7]
            for r in range(7):
                chosen = jnp.where(want == r, blocks[r], chosen)
            if i == 0:
                pcol[s, y] = chosen
            else:
                psend[s, i] = chosen
                col_copy(s, i, y).start()

    def halos(s):
        for e in (0, 1):
            halo_copy(s, e).wait_recv()
        for c in range(COMP):
            win[s, c, TOP - 2 : TOP, :] = halo[s, 0, 2 * c : 2 * c + 2, :]
            win[s, c, TOP + ROWS : TOP + ROWS + 2, :] = halo[s, 1, 2 * c : 2 * c + 2, :]
        for j in (0, 3):
            faces(s, j)

    def finish(s, j):
        rows = pl.ds(8 * j, 8)
        z_copy(s, j).wait_recv()
        right = [
            grad[b, rows, :] - summed[b, rows, :] - (own[b, rows, :] + zrecv[s, b, rows, :]) for b in range(COMP)
        ]
        value = apply_inverse(rows, right)
        if s + 1 < ITERS:
            publish(s + 1, j, value)
        else:
            for c in range(COMP):
                if j == 0:
                    out_ref[c, 2:8, :] = value[c][2:]
                else:
                    out_ref[c, rows, :] = value[c]

    def finish_first(s, upper):
        for i in range(1, 8):
            col_copy(s, i, lax.rem(y + i, 8)).wait_recv()
        mine = tab[8]
        want = jnp.broadcast_to((mine >> 1) & 7, (16, 128))
        source = pcol[s, 7]
        for r in range(7):
            source = jnp.where(want == r, pcol[s, r], source)
        terms = []
        for b in range(COMP):
            term = grad[b, 0:2, :] - summed[b, 0:2, :]
            for a in range(COMP):
                term = term - plane[a, b].astype(F32) * source[2 * a : 2 * a + 2]
            terms.append(term)
        if upper:
            near_arrivals(s)
            first_copy(s).wait_recv()
            coupled = [first_sum(s, 0, 1, h) + zgot[s, 8 * h : 8 * h + 8, :] for h in (0, 1)]
        else:
            for other in range(4):
                cross_copy(s, other, (1 - half) * 4 + other).wait_recv()
            coupled = [first_sum(s, 0, 0, h) + first_sum(s, 1, 1, h) for h in (0, 1)]
        coupled = [coupled[b // 4][2 * b % 8 : 2 * b % 8 + 2] for b in range(COMP)]
        first = pl.ds(0, 2)
        value = apply_inverse(first, [terms[b] - coupled[b] for b in range(COMP)])
        if s + 1 < ITERS:
            publish_first(s + 1, value)
        else:
            for c in range(COMP):
                out_ref[c, 0:2, :] = value[c]

    def drain(s):
        if s == 0:
            for i in range(1, 8):
                tab_copy(i, y).wait_send()
        for j in range(CHUNKS):
            for i in (1, 2, 3):
                x_copy(s, i, j).wait_send()
            z_copy(s, j).wait_send()
        for e in (0, 1):
            halo_copy(s, e).wait_send()

        @pl.when(half == 0)
        def _():
            first_copy(s).wait_send()

        @pl.when(half == 1)
        def _():
            for other in range(4):
                cross_copy(s, other, q).wait_send()

        for i in (1, 2, 3):
            near_copy(s, i, q).wait_send()
        for i in range(1, 8):
            row_copy(s, i, col).wait_send()
            col_copy(s, i, y).wait_send()

    @pl.when(half == 0)
    def _():
        for j in (1, 2):
            faces(0, j)
        select(0)
        for j in range(CHUNKS):
            instances(0, j, send=False)
        first_across(0)
        pl.semaphore_wait(met_sem, 1)
        first_copy(0).start()
        for j in range(CHUNKS):
            z_copy(0, j).start()
        halos(0)
        finish_first(0, False)
        for j in range(CHUNKS):
            finish(0, j)
        for j in (1, 2):
            faces(1, j)
        select(1)
        first_across(1)
        first_copy(1).start()
        for j in range(CHUNKS):
            instances(1, j)
        drain(0)
        halos(1)
        drain(1)
        finish_first(1, False)
        for j in range(CHUNKS):
            finish(1, j)

    @pl.when(half == 1)
    def _():
        for j in (1, 2):
            faces(0, j)
        for j in (0, 1):
            instances(0, j)
        select(0)
        for j in (2, 3):
            instances(0, j)
        halos(0)
        for j in range(CHUNKS):
            finish(0, j)
        finish_first(0, True)
        for j in (1, 2):
            faces(1, j)
        for j in range(CHUNKS):
            instances(1, j)
        drain(0)
        select(1)
        halos(1)
        drain(1)
        finish_first(1, True)
        for j in range(CHUNKS):
            finish(1, j)


def body(objective_grad, face_jacobians, plane_jacobians, diagonal_inverse, neighbours, plane_source):
    blocks = ROWS // 2
    grad = objective_grad.reshape(2, COMP, blocks, 128).transpose(1, 2, 0, 3).reshape(COMP, ROWS, 128)
    face = face_jacobians.reshape(2, FACES, COMP, COMP, blocks, 128)
    face = face.transpose(1, 2, 3, 4, 0, 5).reshape(FACES, COMP, COMP, ROWS, 128)
    inv = diagonal_inverse.reshape(2, COMP, COMP, blocks, 128)
    inv = inv.transpose(1, 2, 3, 0, 4).reshape(COMP, COMP, ROWS, 128)
    plane = plane_jacobians.transpose(1, 2, 0, 3)
    anywhere = pl.BlockSpec(memory_space=pl.ANY)
    dma = pltpu.SemaphoreType.DMA
    out = pl.pallas_call(
        kernel,
        out_shape=jax.ShapeDtypeStruct((COMP, ROWS, 128), F32),
        in_specs=[anywhere] * 5 + [pl.BlockSpec(memory_space=pltpu.SMEM)],
        out_specs=pl.BlockSpec(memory_space=pltpu.VMEM),
        scratch_shapes=[
            pltpu.VMEM((COMP, ROWS, 128), F32),
            pltpu.VMEM((FACES, COMP, COMP, ROWS, 128), jnp.bfloat16),
            pltpu.VMEM((COMP, COMP, 2, 128), jnp.bfloat16),
            pltpu.VMEM((COMP, COMP, ROWS, 128), F32),
            pltpu.VMEM((FACES, 2048), jnp.int32),
            pltpu.VMEM((FACES, ROWS, 128), jnp.int32),
            pltpu.VMEM((FACES, ROWS, 128), jnp.int32),
            pltpu.VMEM((ITERS + 1, COMP, ROWS + 2 * TOP, 128), F32),
            pltpu.VMEM((COMP, ROWS, 128), F32),
            pltpu.VMEM((COMP, ROWS, 128), F32),
            pltpu.VMEM((ITERS, 4, COMP, ROWS, 128), F32),
            pltpu.VMEM((ITERS, COMP, ROWS, 128), F32),
            pltpu.VMEM((ITERS, COMP, ROWS, 128), F32),
            pltpu.VMEM((ITERS, 2, 16, 128), F32),
            pltpu.VMEM((ITERS, 2, 16, 128), F32),
            pltpu.VMEM((ITERS, 8, 16, 128), F32),
            pltpu.VMEM((ITERS, 8, 16, 128), F32),
            pltpu.VMEM((ITERS, 8, 16, 128), F32),
            pltpu.VMEM((ITERS, 8, 16, 128), F32),
            pltpu.VMEM((ITERS, 16, 128), F32),
            pltpu.VMEM((ITERS, 16, 128), F32),
            pltpu.VMEM((9, 1, 128), jnp.int32),
            dma((5,)),
            dma((ITERS, 4, CHUNKS)), dma((ITERS, 4, CHUNKS)),
            dma((ITERS, CHUNKS)), dma((ITERS, CHUNKS)),
            dma((ITERS, 2)), dma((ITERS, 2)),
            dma((ITERS, 8)), dma((ITERS, 8)),
            dma((ITERS, 8)), dma((ITERS, 8)),
            dma((ITERS, 8)), dma((ITERS, 8)),
            dma((8,)), dma((8,)),
            pltpu.SemaphoreType.REGULAR,
            pltpu.SemaphoreType.REGULAR,
            dma((ITERS,)), dma((ITERS,)),
        ],
        compiler_params=pltpu.CompilerParams(
            collective_id=0, has_side_effects=True, vmem_limit_bytes=60 * 1024 * 1024
        ),
    )(grad, face, plane, inv, neighbours, plane_source)
    return out.reshape(COMP, blocks, 2, 128).transpose(2, 0, 1, 3).reshape(2, COMP, 2048)


def solution(mesh):
    placed = (
        P("inst", None, "space"),
        P("inst", None, None, None, "space"),
        P("inst", None, None, "space"),
        P("inst", None, None, "space"),
        P(None, "space"),
        P("space"),
    )
    return jax.shard_map(
        body, mesh=mesh, in_specs=placed, out_specs=P("inst", None, "space"), check_vma=False
    )
```

```python
import functools
import math

import jax
import jax.numpy as jnp
from jax import lax
from jax.experimental import pallas as pl
from jax.experimental.pallas import tpu as pltpu
from jax.sharding import PartitionSpec as P

MESH = pl.DeviceIdType.MESH
F32 = jnp.float32

ITERS = 2
NT = 16
COMP = 5
FACES = 6
FREQUENCY = 0.05

ROWS = 32
CHUNKS = 4
TOP = 8


def spectral(diff):
    diff = diff % NT
    if diff == 0:
        return 0.0
    return FREQUENCY * 0.5 * (-1.0) ** diff / math.tan(math.pi * diff / NT)


def pick(position, values):
    out = jnp.float32(values[-1])
    for i in range(len(values) - 1):
        out = jnp.where(position == i, jnp.float32(values[i]), out)
    return out


def kernel(
    grad_hbm, face_hbm, plane_hbm, inv_hbm, nb_hbm, src_ref, out_ref,
    grad, face, plane, inv, nb, lane, side, win, summed, own, xbuf, zsend, zrecv,
    edge, halo, prow, psend, pcol, ibuf, zfirst, zgot, tab,
    load_sem, xs_sem, xr_sem, zs_sem, zr_sem, hs_sem, hr_sem, as_sem, ar_sem, bs_sem, br_sem, is_sem, ir_sem, ts_sem, tr_sem, met_sem, mate_sem, fs_sem, fr_sem,
):
    q, d = lax.axis_index("inst"), lax.axis_index("space")
    half, x = q // 4, lax.rem(q, 4)
    zlo, y, core = d // 16, lax.rem(d, 16) // 2, lax.rem(d, 2)
    col = zlo * 2 + core

    loads = [
        pltpu.make_async_copy(src, dst, load_sem.at[i])
        for i, (src, dst) in enumerate(
            [(grad_hbm, grad), (inv_hbm, inv), (nb_hbm, nb), (plane_hbm, plane), (face_hbm, face)]
        )
    ]
    for load in loads:
        load.start()

    def x_peer(i):
        return (half * 4 + lax.rem(x + i, 4), d)

    z_peer = (lax.rem(q + 4, 8), d)

    before, after = (q, lax.rem(d + 63, 64)), (q, lax.rem(d + 1, 64))

    def y_peer(i):
        return (q, zlo * 16 + lax.rem(y + i, 8) * 2 + core)

    def col_of(i):
        return lax.rem(col + i, 8)

    def col_peer(i):
        other = col_of(i)
        return (q, other // 2 * 16 + y * 2 + lax.rem(other, 2))

    across = [((1 - half) * 4 + other, d) for other in range(4)]
    mate = (q, d + 1 - 2 * core)
    barrier = pltpu.get_barrier_semaphore()

    def greet(p):
        pl.semaphore_signal(barrier, inc=1, device_id=p, device_id_type=MESH)

    def even(p):
        return (p[0], p[1] - lax.rem(p[1], 2))

    def odd_one(p):
        return (p[0], p[1] - lax.rem(p[1], 2) + 1)

    for i in (1, 2, 3):
        greet(even(x_peer(i)))

    @pl.when(core == 1)
    def _():
        greet(mate)

    @pl.when(half == 0)
    def _():
        for p in across:
            greet(even(p))

    greet(odd_one(after))
    for i in range(1, 8):
        greet(odd_one(y_peer(i)))
    for i in range(2, 7):
        greet(odd_one(col_peer(i)))

    @pl.when(core == 0)
    def _():
        greet(odd_one(before))
        greet(odd_one(col_peer(1)))
        greet(odd_one(col_peer(7)))

    @pl.when(core == 1)
    def _():
        greet(odd_one(col_peer(1)))

    def tell_mate():
        pl.semaphore_signal(mate_sem, inc=1, device_id=mate, device_id_type=MESH)

    def enter_inst():
        @pl.when(core == 0)
        def _():
            @pl.when(half == 0)
            def _():
                pl.semaphore_wait(barrier, 7)

            @pl.when(half == 1)
            def _():
                pl.semaphore_wait(barrier, 15)
                pl.semaphore_signal(met_sem, inc=1, device_id=z_peer, device_id_type=MESH)
                pl.semaphore_signal(met_sem, inc=1, device_id=(z_peer[0], d + 1), device_id_type=MESH)

            tell_mate()

        @pl.when(core == 1)
        def _():
            pl.semaphore_wait(mate_sem, 1)

    def enter_space():
        @pl.when(core == 1)
        def _():
            pl.semaphore_wait(barrier, 30)
            tell_mate()

        @pl.when(core == 0)
        def _():
            pl.semaphore_wait(mate_sem, 1)

    def x_copy(s, i, j):
        rows = pl.ds(8 * j, 8)
        return pltpu.make_async_remote_copy(
            src_ref=xbuf.at[s, x, :, rows], dst_ref=xbuf.at[s, x, :, rows],
            send_sem=xs_sem.at[s, i, j], recv_sem=xr_sem.at[s, x, j],
            device_id=x_peer(i), device_id_type=MESH,
        )

    def x_arrival(s, i, j):
        rows, slot = pl.ds(8 * j, 8), lax.rem(x + i, 4)
        return pltpu.make_async_remote_copy(
            src_ref=xbuf.at[s, slot, :, rows], dst_ref=xbuf.at[s, slot, :, rows],
            send_sem=xs_sem.at[s, i, j], recv_sem=xr_sem.at[s, slot, j],
            device_id=x_peer(i), device_id_type=MESH,
        )

    def z_copy(s, j):
        rows = pl.ds(8 * j, 8)
        return pltpu.make_async_remote_copy(
            src_ref=zsend.at[s, :, rows], dst_ref=zrecv.at[s, :, rows],
            send_sem=zs_sem.at[s, j], recv_sem=zr_sem.at[s, j],
            device_id=z_peer, device_id_type=MESH,
        )

    def halo_copy(s, e):
        return pltpu.make_async_remote_copy(
            src_ref=edge.at[s, e], dst_ref=halo.at[s, 1 - e],
            send_sem=hs_sem.at[s, e], recv_sem=hr_sem.at[s, 1 - e],
            device_id=after if e else before, device_id_type=MESH,
        )

    def row_copy(s, i, slot):
        return pltpu.make_async_remote_copy(
            src_ref=edge.at[s, 0], dst_ref=prow.at[s, slot],
            send_sem=as_sem.at[s, i], recv_sem=ar_sem.at[s, slot],
            device_id=col_peer(i), device_id_type=MESH,
        )

    def col_copy(s, i, slot):
        return pltpu.make_async_remote_copy(
            src_ref=psend.at[s, i], dst_ref=pcol.at[s, slot],
            send_sem=bs_sem.at[s, i], recv_sem=br_sem.at[s, slot],
            device_id=y_peer(i), device_id_type=MESH,
        )

    def tab_copy(i, slot):
        return pltpu.make_async_remote_copy(
            src_ref=tab.at[8], dst_ref=tab.at[slot],
            send_sem=ts_sem.at[i], recv_sem=tr_sem.at[slot],
            device_id=y_peer(i), device_id_type=MESH,
        )

    odd = lax.rem(lax.broadcasted_iota(jnp.int32, (8, 128), 0), 2) == 1
    coef = []
    for base in (0, 8):
        straight, crossed = [], []
        for other in range(4):
            steps = [2 * (other - me) + base for me in range(4)]
            straight.append(pick(x, [spectral(e) for e in steps]))
            crossed.append(
                jnp.where(odd, pick(x, [spectral(e + 1) for e in steps]), pick(x, [spectral(e - 1) for e in steps]))
            )
        coef.append((straight, crossed))

    def swap(v, mask):
        return jnp.where(mask, pltpu.roll(v, 1, 0), pltpu.roll(v, v.shape[0] - 1, 0))

    def cross_copy(s, other, slot):
        return pltpu.make_async_remote_copy(
            src_ref=edge.at[s, 0], dst_ref=ibuf.at[s, slot],
            send_sem=is_sem.at[s, other], recv_sem=ir_sem.at[s, slot],
            device_id=across[other], device_id_type=MESH,
        )

    def near_copy(s, i, slot):
        return pltpu.make_async_remote_copy(
            src_ref=edge.at[s, 0], dst_ref=ibuf.at[s, slot],
            send_sem=is_sem.at[s, 4 + i], recv_sem=ir_sem.at[s, slot],
            device_id=x_peer(i), device_id_type=MESH,
        )

    def send_across(s):
        for other in range(4):
            cross_copy(s, other, q).start()

    def send_first(s):
        pl.when(half == 1)(lambda: send_across(s))
        for i in (2, 1, 3):
            near_copy(s, i, q).start()

    def first_copy(s):
        return pltpu.make_async_remote_copy(
            src_ref=zfirst.at[s], dst_ref=zgot.at[s], send_sem=fs_sem.at[s], recv_sem=fr_sem.at[s],
            device_id=z_peer, device_id_type=MESH,
        )

    def first_sum(s, kind, group, h):
        straight, crossed = coef[kind]
        rows = pl.ds(8 * h, 8)
        values = [ibuf[s, 4 * group + other, rows, :] for other in range(4)]
        plain, turned = straight[0] * values[0], crossed[0] * values[0]
        for other in range(1, 4):
            plain = plain + straight[other] * values[other]
            turned = turned + crossed[other] * values[other]
        return plain + swap(turned, odd)

    def near_arrivals(s):
        for i in (1, 3, 2):
            near_copy(s, i, half * 4 + lax.rem(x + i, 4)).wait_recv()

    def first_across(s):
        near_arrivals(s)
        for h in (0, 1):
            zfirst[s, 8 * h : 8 * h + 8, :] = first_sum(s, 1, 0, h)

    def publish_first(s, value):
        for c in range(COMP):
            win[s, c, TOP : TOP + 2, :] = value[c]
            edge[s, 0, 2 * c : 2 * c + 2, :] = value[c]
        if s:
            send_first(s)
            send_space(s, 0)
        block = edge[s, 0]
        ibuf[s, q] = block
        prow[s, col] = block

    def send_space(s, e):
        if e == 0:
            for i in (4, 3, 5, 2, 6, 1, 7):
                row_copy(s, i, col).start()
        halo_copy(s, e).start()

    def publish(s, j, value):
        for c in range(COMP):
            if j == 0:
                win[s, c, TOP + 2 : TOP + 8, :] = value[c][2:]
            else:
                win[s, c, pl.ds(TOP + 8 * j, 8), :] = value[c]
            xbuf[s, x, c, pl.ds(8 * j, 8), :] = value[c]
        for i in (2, 1, 3):
            x_copy(s, i, j).start()
        if j == CHUNKS - 1:
            for c in range(COMP):
                edge[s, 1, 2 * c : 2 * c + 2, :] = value[c][6:8]
            if s:
                send_space(s, 1)

    def apply_inverse(rows, values):
        out = []
        for c in range(COMP):
            total = inv[0, c, rows, :] * values[0]
            for b in range(1, COMP):
                total = total + inv[b, c, rows, :] * values[b]
            out.append(total)
        return out

    def faces(s, j):
        rows = pl.ds(8 * j, 8)
        tall = pl.ds(16 * (j // 2), 16)
        lower = 8 * (j % 2)

        def one_face(k, total):
            at, where = lane[k, rows, :], side[k, rows, :]
            total = list(total)
            for a in range(COMP):
                got = [
                    jnp.take_along_axis(
                        win[s, a, pl.ds(TOP + 8 * j + 2 * o, 8), :], at, axis=1, mode="promise_in_bounds"
                    )
                    for o in (-1, 0, 1)
                ]
                beside = jnp.where(where == 0, got[0], jnp.where(where == 1, got[1], got[2]))
                for b in range(COMP):
                    jac = face[k, a, b, tall, :].astype(F32)[lower : lower + 8]
                    total[b] = total[b] + jac * beside
            return tuple(total)

        total = lax.fori_loop(0, FACES, one_face, tuple(jnp.zeros((8, 128), F32) for _ in range(COMP)), unroll=True)
        for b in range(COMP):
            summed[b, rows, :] = total[b]

    def instances(s, j, send=True):
        rows = pl.ds(8 * j, 8)
        for i in (1, 3, 2):
            x_arrival(s, i, j).wait_recv()
        for a in range(COMP):
            values = [xbuf[s, other, a, rows, :] for other in range(4)]
            sums = []
            for straight, crossed in coef:
                plain = straight[0] * values[0]
                turned = crossed[0] * values[0]
                for other in range(1, 4):
                    plain = plain + straight[other] * values[other]
                    turned = turned + crossed[other] * values[other]
                sums.append(plain + swap(turned, odd))
            own[a, rows, :] = sums[0]
            zsend[s, a, rows, :] = sums[1]
        if send:
            z_copy(s, j).start()

    tab[8] = jnp.full((1, 128), src_ref[0], jnp.int32)
    tab[y] = jnp.full((1, 128), src_ref[0], jnp.int32)
    enter_inst()
    loads[0].wait()
    loads[1].wait()
    for j in range(CHUNKS):
        value = apply_inverse(pl.ds(8 * j, 8), [grad[b, pl.ds(8 * j, 8), :] for b in range(COMP)])
        if j == 0:
            publish_first(0, [v[0:2] for v in value])
            send_first(0)
        if j == 0:
            enter_space()
            send_space(0, 0)
        publish(0, j, value)

    send_space(0, 1)
    for i in range(1, 8):
        tab_copy(i, y).start()
    loads[2].wait()
    for k in range(FACES):
        for block in range(ROWS // 2):
            index = nb[k : k + 1, 128 * block : 128 * block + 128] - 128 * block
            lane[k, 2 * block : 2 * block + 2, :] = jnp.broadcast_to(index & 127, (2, 128))
            side[k, 2 * block : 2 * block + 2, :] = jnp.broadcast_to(index >> 7, (2, 128))
    loads[3].wait()
    loads[4].wait()

    def select(s):
        for i in range(1, 8):
            row_copy(s, i, col_of(i)).wait_recv()
        if s == 0:
            for i in range(1, 8):
                tab_copy(i, lax.rem(y + i, 8)).wait_recv()
        blocks = [prow[s, r] for r in range(8)]
        for i in (4, 3, 5, 2, 6, 1, 7, 0):
            wanted = tab[lax.rem(y + i, 8)]
            want = jnp.broadcast_to((wanted >> 4) * 2 + (wanted & 1), (16, 128))
            chosen = blocks[7]
            for r in range(7):
                chosen = jnp.where(want == r, blocks[r], chosen)
            if i == 0:
                pcol[s, y] = chosen
            else:
                psend[s, i] = chosen
                col_copy(s, i, y).start()

    def halos(s):
        for e in (0, 1):
            halo_copy(s, e).wait_recv()
        for c in range(COMP):
            win[s, c, TOP - 2 : TOP, :] = halo[s, 0, 2 * c : 2 * c + 2, :]
            win[s, c, TOP + ROWS : TOP + ROWS + 2, :] = halo[s, 1, 2 * c : 2 * c + 2, :]
        for j in (0, 3):
            faces(s, j)

    def finish(s, j):
        rows = pl.ds(8 * j, 8)
        z_copy(s, j).wait_recv()
        right = [
            grad[b, rows, :] - summed[b, rows, :] - (own[b, rows, :] + zrecv[s, b, rows, :]) for b in range(COMP)
        ]
        value = apply_inverse(rows, right)
        if s + 1 < ITERS:
            publish(s + 1, j, value)
        else:
            for c in range(COMP):
                if j == 0:
                    out_ref[c, 2:8, :] = value[c][2:]
                else:
                    out_ref[c, rows, :] = value[c]

    def finish_first(s, upper):
        for i in range(1, 8):
            col_copy(s, i, lax.rem(y + i, 8)).wait_recv()
        mine = tab[8]
        want = jnp.broadcast_to((mine >> 1) & 7, (16, 128))
        source = pcol[s, 7]
        for r in range(7):
            source = jnp.where(want == r, pcol[s, r], source)
        terms = []
        for b in range(COMP):
            term = grad[b, 0:2, :] - summed[b, 0:2, :]
            for a in range(COMP):
                term = term - plane[a, b].astype(F32) * source[2 * a : 2 * a + 2]
            terms.append(term)
        if upper:
            near_arrivals(s)
            first_copy(s).wait_recv()
            coupled = [first_sum(s, 0, 1, h) + zgot[s, 8 * h : 8 * h + 8, :] for h in (0, 1)]
        else:
            for other in range(4):
                cross_copy(s, other, (1 - half) * 4 + other).wait_recv()
            coupled = [first_sum(s, 0, 0, h) + first_sum(s, 1, 1, h) for h in (0, 1)]
        coupled = [coupled[b // 4][2 * b % 8 : 2 * b % 8 + 2] for b in range(COMP)]
        first = pl.ds(0, 2)
        value = apply_inverse(first, [terms[b] - coupled[b] for b in range(COMP)])
        if s + 1 < ITERS:
            publish_first(s + 1, value)
        else:
            for c in range(COMP):
                out_ref[c, 0:2, :] = value[c]

    def drain(s):
        if s == 0:
            for i in range(1, 8):
                tab_copy(i, y).wait_send()
        for j in range(CHUNKS):
            for i in (1, 2, 3):
                x_copy(s, i, j).wait_send()
            z_copy(s, j).wait_send()
        for e in (0, 1):
            halo_copy(s, e).wait_send()

        @pl.when(half == 0)
        def _():
            first_copy(s).wait_send()

        @pl.when(half == 1)
        def _():
            for other in range(4):
                cross_copy(s, other, q).wait_send()

        for i in (1, 2, 3):
            near_copy(s, i, q).wait_send()
        for i in range(1, 8):
            row_copy(s, i, col).wait_send()
            col_copy(s, i, y).wait_send()

    @pl.when(half == 0)
    def _():
        for j in (1, 2):
            faces(0, j)
        select(0)
        for j in range(CHUNKS):
            instances(0, j, send=False)
        first_across(0)
        pl.semaphore_wait(met_sem, 1)
        first_copy(0).start()
        for j in range(CHUNKS):
            z_copy(0, j).start()
        halos(0)
        finish_first(0, False)
        for j in range(CHUNKS):
            finish(0, j)
        for j in (1, 2):
            faces(1, j)
        select(1)
        first_across(1)
        first_copy(1).start()
        for j in range(CHUNKS):
            instances(1, j)
        drain(0)
        halos(1)
        drain(1)
        finish_first(1, False)
        for j in range(CHUNKS):
            finish(1, j)

    @pl.when(half == 1)
    def _():
        for j in (1, 2):
            faces(0, j)
        for j in (0, 1):
            instances(0, j)
        select(0)
        for j in (2, 3):
            instances(0, j)
        halos(0)
        for j in range(CHUNKS):
            finish(0, j)
        finish_first(0, True)
        for j in (1, 2):
            faces(1, j)
        for j in range(CHUNKS):
            instances(1, j)
        drain(0)
        select(1)
        halos(1)
        drain(1)
        finish_first(1, True)
        for j in range(CHUNKS):
            finish(1, j)


def body(objective_grad, face_jacobians, plane_jacobians, diagonal_inverse, neighbours, plane_source):
    blocks = ROWS // 2
    grad = objective_grad.reshape(2, COMP, blocks, 128).transpose(1, 2, 0, 3).reshape(COMP, ROWS, 128)
    face = face_jacobians.reshape(2, FACES, COMP, COMP, blocks, 128)
    face = face.transpose(1, 2, 3, 4, 0, 5).reshape(FACES, COMP, COMP, ROWS, 128)
    inv = diagonal_inverse.reshape(2, COMP, COMP, blocks, 128)
    inv = inv.transpose(1, 2, 3, 0, 4).reshape(COMP, COMP, ROWS, 128)
    plane = plane_jacobians.transpose(1, 2, 0, 3)
    anywhere = pl.BlockSpec(memory_space=pl.ANY)
    dma = pltpu.SemaphoreType.DMA
    out = pl.pallas_call(
        kernel,
        out_shape=jax.ShapeDtypeStruct((COMP, ROWS, 128), F32),
        in_specs=[anywhere] * 5 + [pl.BlockSpec(memory_space=pltpu.SMEM)],
        out_specs=pl.BlockSpec(memory_space=pltpu.VMEM),
        scratch_shapes=[
            pltpu.VMEM((COMP, ROWS, 128), F32),
            pltpu.VMEM((FACES, COMP, COMP, ROWS, 128), jnp.bfloat16),
            pltpu.VMEM((COMP, COMP, 2, 128), jnp.bfloat16),
            pltpu.VMEM((COMP, COMP, ROWS, 128), F32),
            pltpu.VMEM((FACES, 2048), jnp.int32),
            pltpu.VMEM((FACES, ROWS, 128), jnp.int32),
            pltpu.VMEM((FACES, ROWS, 128), jnp.int32),
            pltpu.VMEM((ITERS + 1, COMP, ROWS + 2 * TOP, 128), F32),
            pltpu.VMEM((COMP, ROWS, 128), F32),
            pltpu.VMEM((COMP, ROWS, 128), F32),
            pltpu.VMEM((ITERS, 4, COMP, ROWS, 128), F32),
            pltpu.VMEM((ITERS, COMP, ROWS, 128), F32),
            pltpu.VMEM((ITERS, COMP, ROWS, 128), F32),
            pltpu.VMEM((ITERS, 2, 16, 128), F32),
            pltpu.VMEM((ITERS, 2, 16, 128), F32),
            pltpu.VMEM((ITERS, 8, 16, 128), F32),
            pltpu.VMEM((ITERS, 8, 16, 128), F32),
            pltpu.VMEM((ITERS, 8, 16, 128), F32),
            pltpu.VMEM((ITERS, 8, 16, 128), F32),
            pltpu.VMEM((ITERS, 16, 128), F32),
            pltpu.VMEM((ITERS, 16, 128), F32),
            pltpu.VMEM((9, 1, 128), jnp.int32),
            dma((5,)),
            dma((ITERS, 4, CHUNKS)), dma((ITERS, 4, CHUNKS)),
            dma((ITERS, CHUNKS)), dma((ITERS, CHUNKS)),
            dma((ITERS, 2)), dma((ITERS, 2)),
            dma((ITERS, 8)), dma((ITERS, 8)),
            dma((ITERS, 8)), dma((ITERS, 8)),
            dma((ITERS, 8)), dma((ITERS, 8)),
            dma((8,)), dma((8,)),
            pltpu.SemaphoreType.REGULAR,
            pltpu.SemaphoreType.REGULAR,
            dma((ITERS,)), dma((ITERS,)),
        ],
        compiler_params=pltpu.CompilerParams(
            collective_id=0, has_side_effects=True, vmem_limit_bytes=60 * 1024 * 1024
        ),
    )(grad, face, plane, inv, neighbours, plane_source)
    return out.reshape(COMP, blocks, 2, 128).transpose(2, 0, 1, 3).reshape(2, COMP, 2048)


def solution(mesh):
    placed = (
        P("inst", None, "space"),
        P("inst", None, None, None, "space"),
        P("inst", None, None, "space"),
        P("inst", None, None, "space"),
        P(None, "space"),
        P("space"),
    )
    return jax.shard_map(
        body, mesh=mesh, in_specs=placed, out_specs=P("inst", None, "space"), check_vma=False
    )
```
